128 devices in a mesh: lon: 16 (over x, y_hi, core), lat: 8 (over z, y_lo).
Axes of the slice: x: 4, y: 4 (y_hi: 2, y_lo: 2; y = y_hi * 2 + y_lo), z: 4, core: 2. Of those that a mesh axis runs over, the one named last changes fastest.
Arguments:
- features: bfloat16 [128, 64, 4096], P(None, 'lat', 'lon'), may hold values from -45 to 45
- coarse_blocks: bfloat16 [16, 128, 40, 256], P('lon', 'lat'), may hold values from -6 to 6
- send_table: int32 [16, 8, 8, 8], P('lon'), may hold values from -1 to 15, as said below
- interp_src: int32 [2, 64, 4096], P(None, 'lat', 'lon'), may hold values from 0 to 16383, as said below
- interp_wt: float32 [2, 64, 4096], P(None, 'lat', 'lon'), may hold values from 0.25 to 1
- weight_in: bfloat16 [9, 128, 168], replicated, may hold values from -0.15625 to 0.15625
- weight_mid: bfloat16 [9, 128, 128], replicated, may hold values from -0.1875 to 0.1875
- weight_out: bfloat16 [9, 128, 128], replicated, may hold values from -0.1875 to 0.1875
- gain_in: float32 [128], replicated, may hold values from 0.5 to 2
- bias_in: float32 [128], replicated, may hold values from -3 to 3
- gain_mid: float32 [128], replicated, may hold values from 0.5 to 2
- bias_mid: float32 [128], replicated, may hold values from -3 to 3
- cotangent: bfloat16 [128, 64, 4096], P(None, 'lat', 'lon'), may hold values from -6 to 6
Outputs:
- output_field: bfloat16 [128, 64, 4096], P(None, 'lat', 'lon')
- grad_features: bfloat16 [128, 64, 4096], P(None, 'lat', 'lon')
- grad_weight_in: float32 [9, 128, 168], replicated
- grad_weight_mid: float32 [9, 128, 128], replicated
- grad_weight_out: float32 [9, 128, 128], replicated
The draws below stay inside these ranges and needn't reach their ends.
Inputs may be any that keep to these rules, and one draw needn't show every extreme that they name: `send_table`: for column j, owner row o and destination row i the used slots come first and hold distinct block indices, the rest are -1; rows more than half of 8 apart exchange nothing, and an owner always fills all 8 slots for its own row. `interp_src`: every index points at a used slot of the cell's own pool.
All inputs are finite; a program needn't handle non-finite values.
Results may differ from the reference program's by a relative error of at most 0.014.
Values may be sent and summed in bfloat16 or wider, within the bound.
A program may use at most 64 MiB of HBM per device.

```python
import math
import jax
import jax.numpy as jnp
from jax import lax

C = 128
CC = 40
G = 32
TILE_LAT = 8
TILE_LON = 256
BS = 256
CB_DEV = 16
SLOT = 8
NLAT = 64
NLON = 4096
CB = 128
N_LON = 16
N_LAT = 8


def owner_counts(key):
    key = jax.random.fold_in(key, 7)
    lat_rows = jnp.arange(N_LAT)
    row_gap = jnp.abs(lat_rows[:, None] - lat_rows[None, :])
    chosen = jax.random.randint(key, (N_LON, N_LAT, N_LAT), 2, SLOT + 1)
    return jnp.where(row_gap[None] == 0, SLOT, jnp.where(row_gap[None] <= N_LAT // 2, chosen, 0)).astype(jnp.int32)


def draw_send_table(key, part):
    counts = owner_counts(key)
    key = jax.random.fold_in(key, 11)
    scores = jax.random.randint(key, (N_LON, N_LAT, N_LAT, CB_DEV), 0, 1 << 20) * CB_DEV + jnp.arange(CB_DEV)
    lat_rows = jnp.arange(N_LAT)
    own_row = (lat_rows[:, None] == lat_rows[None, :])[None, :, :, None]
    scores = jnp.where(own_row & (jnp.arange(CB_DEV) == CB_DEV - 1)[None, None, None, :], -1, scores)
    ranked = jnp.argsort(scores, axis=-1)[..., :SLOT]
    in_use = jnp.arange(SLOT)[None, None, None, :] < counts[..., None]
    return jnp.where(in_use, ranked, -1).astype(jnp.int32)


def draw_interp_src(key, part):
    counts = owner_counts(key)
    key = jax.random.fold_in(key, 13)
    key_pick, key_cell = jax.random.split(key)
    row_dev = jnp.arange(NLAT) // TILE_LAT
    col_dev = jnp.arange(NLON) // TILE_LON
    per_owner = counts[col_dev[None, :], :, row_dev[:, None]]
    upper_ends = jnp.cumsum(per_owner, axis=-1)
    starts = upper_ends - per_owner
    totals = upper_ends[..., -1]
    drawn = jax.random.randint(key_pick, (2, NLAT, NLON), 0, totals[None])
    owners = jnp.sum((upper_ends[None] <= drawn[..., None]).astype(jnp.int32), axis=-1)
    start_full = jnp.broadcast_to(starts[None], (2,) + starts.shape)
    slot_ids = drawn - jnp.take_along_axis(start_full, owners[..., None], axis=-1)[..., 0]
    cell_ids = jax.random.randint(key_cell, (2, NLAT, NLON), 0, BS)
    pool_index = (owners * SLOT + slot_ids) * BS + cell_ids
    lat_pos = jnp.arange(NLAT) % TILE_LAT
    lon_pos = jnp.arange(NLON) % TILE_LON
    first_cell = (lat_pos[:, None] == 0) & (lon_pos[None, :] == 0)
    last_cell = (lat_pos[:, None] == TILE_LAT - 1) & (lon_pos[None, :] == TILE_LON - 1)
    own_first = jnp.broadcast_to((row_dev * SLOT * BS)[:, None], (NLAT, NLON))
    own_last = jnp.broadcast_to(((row_dev * SLOT + SLOT - 1) * BS + BS - 1)[:, None], (NLAT, NLON))
    upper_src = jnp.where(last_cell, own_last, pool_index[0])
    lower_src = jnp.where(first_cell, own_first, pool_index[1])
    return jnp.stack([upper_src, lower_src]).astype(jnp.int32)


def smooth_waves(key, lat_pos, lon_pos):
    key_freq, key_tilt, key_phase = jax.random.split(key, 3)
    lon_freq = jax.random.randint(key_freq, (4,), 1, 9).astype(jnp.float32)
    lat_freq = jax.random.uniform(key_tilt, (4,), minval=0.5, maxval=3.0)
    phases = jax.random.uniform(key_phase, (4,), minval=0.0, maxval=2.0 * math.pi)
    angles = 2.0 * math.pi * (lon_freq[:, None, None] * lon_pos[None, None, :] + lat_freq[:, None, None] * lat_pos[None, :, None]) + phases[:, None, None]
    return jnp.sum(jnp.cos(angles), 0) * math.sqrt(0.5)


def draw_features(key, part):
    key = jax.random.fold_in(key, 3)
    key_base, key_chan, key_common, key_wave = jax.random.split(key, 4)
    lat_pos = jnp.arange(NLAT, dtype=jnp.float32) / max(NLAT - 1, 1)
    lon_pos = jnp.arange(NLON, dtype=jnp.float32) / NLON
    ramp = 1.0 + lat_pos[:, None] + lon_pos[None, :]
    channel_scale = jnp.exp(jax.random.uniform(key_chan, (C, 1, 1), minval=math.log(0.25), maxval=math.log(2.5)))
    smooth = smooth_waves(key_wave, lat_pos, lon_pos)
    rough_common = jax.random.normal(key_common, (NLAT, NLON))
    own_part = jax.random.normal(key_base, (C, NLAT, NLON))
    common = 0.8 * smooth + 0.6 * rough_common
    base_draw = jnp.clip(0.75 * common[None] + 0.66 * own_part, -6.0, 6.0)
    return (base_draw * channel_scale * ramp[None]).astype(jnp.bfloat16)


def levels(stream_key, dims, pieces, low, high):
    def one(axis_at, shards_of):
        draws = jax.random.uniform(jax.random.fold_in(jax.random.fold_in(stream_key, 6), axis_at), (shards_of,), jnp.float32, low / len(pieces), high / len(pieces))
        return jnp.repeat(jnp.exp(draws), dims[axis_at] // shards_of).reshape((-1,) + (1,) * (len(dims) - axis_at - 1))

    factor_of = one(*pieces[0])
    for cut in pieces[1:]:
        factor_of = factor_of * one(*cut)
    return factor_of


def scatter_about(own_key, extent, width, bound, cuts=(), kind=jnp.bfloat16):
    entries = jax.random.normal(own_key, extent, jnp.float32) * width
    if len(cuts) > 0:
        entries = levels(own_key, extent, cuts, -0.22, 0.18) * entries
    return jnp.clip(entries, min=-bound, max=bound).astype(kind)


def setup_inputs(seed: int = 0) -> dict:
    streams_of = jax.random.split(jax.random.key(seed), 14)
    return {
        "features": draw_features(jax.random.fold_in(streams_of[13], 71), 0),
        "coarse_blocks": scatter_about(streams_of[1], (N_LON, CB, CC, BS), 1.0, 6.0, ((0, 16), (1, 8))),
        "send_table": draw_send_table(jax.random.fold_in(streams_of[13], 71), 0),
        "interp_src": draw_interp_src(jax.random.fold_in(streams_of[13], 71), 0),
        "interp_wt": jnp.clip(0.25 + 0.75 * jax.random.uniform(streams_of[4], (2, NLAT, NLON), jnp.float32) ** levels(streams_of[4], (2, NLAT, NLON), ((1, 8), (2, 16)), -0.2, 0.2), 0.25, 1.0),
        "weight_in": scatter_about(streams_of[5], (9, C, C + CC), (9 * (C + CC)) ** -0.5, 0.15625),
        "weight_mid": scatter_about(streams_of[6], (9, C, C), (9 * C) ** -0.5, 0.1875),
        "weight_out": scatter_about(streams_of[7], (9, C, C), (9 * C) ** -0.5, 0.1875),
        "gain_in": jnp.clip(jax.random.uniform(streams_of[8], (C,), jnp.float32, 0.5, 2.0), 0.5, 2.0),
        "bias_in": scatter_about(streams_of[9], (C,), 0.5, 3.0, (), jnp.float32),
        "gain_mid": jnp.clip(jax.random.uniform(streams_of[10], (C,), jnp.float32, 0.5, 2.0), 0.5, 2.0),
        "bias_mid": scatter_about(streams_of[11], (C,), 0.5, 3.0, (), jnp.float32),
        "cotangent": scatter_about(streams_of[12], (C, NLAT, NLON), 1.0, 6.0, ((1, 8), (2, 16))),
    }


def pad_grid(field):
    wrapped = jnp.concatenate([field[:, :, -1:], field, field[:, :, :1]], axis=2)
    return jnp.pad(wrapped, ((0, 0), (1, 1), (0, 0)))

def convolve(padded, weights, height, breadth):
    running = None
    for stencil in range(9):
        row_shift, col_shift = (stencil // 3, stencil % 3)
        window = padded[:, row_shift:row_shift + height, col_shift:col_shift + breadth].reshape(padded.shape[0], -1)
        partial_sum = jnp.dot(weights[stencil], window, preferred_element_type=jnp.float32)
        running = partial_sum if running is None else running + partial_sum
    return running.reshape(weights.shape[1], height, breadth)

def transposed(padded, weights, height, breadth):
    running = None
    for stencil in range(9):
        row_shift, col_shift = (2 - stencil // 3, 2 - stencil % 3)
        window = padded[:, row_shift:row_shift + height, col_shift:col_shift + breadth].reshape(padded.shape[0], -1)
        partial_sum = lax.dot_general(weights[stencil], window, (((0,), (0,)), ((), ())), preferred_element_type=jnp.float32)
        running = partial_sum if running is None else running + partial_sum
    return running.reshape(weights.shape[2], height, breadth)

def correlate(padded, gradient, height, breadth):
    flattened = gradient.reshape(gradient.shape[0], -1)
    stacked = []
    for stencil in range(9):
        row_shift, col_shift = (stencil // 3, stencil % 3)
        window = padded[:, row_shift:row_shift + height, col_shift:col_shift + breadth].reshape(padded.shape[0], -1)
        stacked.append(lax.dot_general(flattened, window, (((1,), (1,)), ((), ())), preferred_element_type=jnp.float32))
    return jnp.stack(stacked)

def group_sums(hidden, groups):
    grouped = hidden.reshape(groups, -1)
    return (lax.optimization_barrier(jnp.sum(grouped, 1)), lax.optimization_barrier(jnp.sum(grouped * grouped, 1)))

def pair_sums(first, second, groups):
    grouped = first.reshape(groups, -1)
    return (lax.optimization_barrier(jnp.sum(grouped, 1)), lax.optimization_barrier(jnp.sum(grouped * second.reshape(groups, -1), 1)))

def normalize(hidden, sums, squares, members, gain, bias):
    groups = sums.shape[0]
    average = sums / members
    variance = squares / members - average * average
    inv_scale = lax.rsqrt(variance + 1e-05)
    grouped = hidden.reshape(groups, -1)
    normed = ((grouped - average[:, None]) * inv_scale[:, None]).reshape(hidden.shape)
    affine = gain[:, None, None] * normed + bias[:, None, None]
    return (normed, affine, inv_scale)

def norm_slope(grad_act, affine, gain):
    squash = jax.nn.sigmoid(affine)
    return grad_act * squash * (1.0 + affine * (1.0 - squash)) * gain[:, None, None]

def finish_back(slope, normed, inv_scale, sum_e, sum_en, members):
    groups = sum_e.shape[0]
    mean_e = sum_e / members
    mean_en = sum_en / members
    grouped = slope.reshape(groups, -1)
    normed_group = normed.reshape(groups, -1)
    result = (grouped - mean_e[:, None] - normed_group * mean_en[:, None]) * inv_scale[:, None]
    return result.reshape(slope.shape).astype(jnp.bfloat16)

def pool_four(field):
    chans, height, breadth = field.shape
    return field.astype(jnp.float32).reshape(chans, height // 4, 4, breadth // 4, 4).mean(axis=(2, 4)).astype(jnp.bfloat16)

def up_four(field):
    return jnp.repeat(jnp.repeat(field, 4, axis=1), 4, axis=2)

def fold_four(field):
    chans, height, breadth = field.shape
    return field.reshape(chans, height // 4, 4, breadth // 4, 4).sum(axis=(2, 4))

def interpolate(coarse_blocks, send_table, interp_src, interp_wt):
    blocks = coarse_blocks.reshape(N_LON, N_LAT, CB_DEV, CC, BS)
    lon_ids = jnp.arange(N_LON)[:, None, None, None]
    lat_ids = jnp.arange(N_LAT)[None, :, None, None]
    picked = blocks[lon_ids, lat_ids, jnp.maximum(send_table, 0)]
    picked = jnp.where((send_table >= 0)[..., None, None], picked, jnp.zeros((), jnp.bfloat16))
    gathered_pool = jnp.transpose(picked, (0, 2, 1, 3, 4, 5)).reshape(-1, CC, BS)
    row_dev = (jnp.arange(NLAT) // TILE_LAT)[:, None]
    col_dev = (jnp.arange(NLON) // TILE_LON)[None, :]
    pool_base = (col_dev * N_LAT + row_dev) * (N_LAT * SLOT)
    block_ids = pool_base[None] + interp_src // BS
    values = gathered_pool[block_ids, :, interp_src % BS]
    blended = lax.optimization_barrier(jnp.sum(interp_wt[..., None] * values.astype(jnp.float32), 0))
    return jnp.transpose(blended, (2, 0, 1)).astype(jnp.bfloat16)

def reference(features, coarse_blocks, send_table, interp_src, interp_wt, weight_in, weight_mid, weight_out, gain_in, bias_in, gain_mid, bias_mid, cotangent):
    condition = interpolate(coarse_blocks, send_table, interp_src, interp_wt)
    inputs = jnp.concatenate([features, condition], axis=0)
    height, breadth = (NLAT, NLON)
    small_h, small_w = (height // 4, breadth // 4)
    members = C // G * height * breadth
    factor = (height * breadth) ** (-0.5)
    pad_in = pad_grid(inputs)
    hidden_in = convolve(pad_in, weight_in, height, breadth)
    sums, squares = group_sums(hidden_in, G)
    normed_in, affine_in, inv_in = normalize(hidden_in, sums, squares, members, gain_in, bias_in)
    act_in = jax.nn.silu(affine_in).astype(jnp.bfloat16)
    pooled = pool_four(act_in)
    pad_mid = pad_grid(pooled)
    hidden_mid = convolve(pad_mid, weight_mid, small_h, small_w)
    sums, squares = group_sums(hidden_mid, G)
    normed_mid, affine_mid, inv_mid = normalize(hidden_mid, sums, squares, members // 16, gain_mid, bias_mid)
    act_mid = jax.nn.silu(affine_mid).astype(jnp.bfloat16)
    merged = (act_in.astype(jnp.float32) + up_four(act_mid).astype(jnp.float32)).astype(jnp.bfloat16)
    pad_out = pad_grid(merged)
    hidden_out = convolve(pad_out, weight_out, height, breadth)
    output_field = (features.astype(jnp.float32) + hidden_out).astype(jnp.bfloat16)
    grad_weight_out = correlate(pad_out, cotangent, height, breadth) * factor
    grad_merged = transposed(pad_grid(cotangent), weight_out, height, breadth)
    grad_small = fold_four(grad_merged)
    slope = norm_slope(grad_small, affine_mid, gain_mid)
    sum_e, sum_en = pair_sums(slope, normed_mid, G)
    grad_mid_pre = finish_back(slope, normed_mid, inv_mid, sum_e, sum_en, members // 16)
    grad_weight_mid = correlate(pad_mid, grad_mid_pre, small_h, small_w) * factor
    grad_pooled = transposed(pad_grid(grad_mid_pre), weight_mid, small_h, small_w)
    grad_act = grad_merged + up_four(grad_pooled) / 16.0
    slope = norm_slope(grad_act, affine_in, gain_in)
    sum_e, sum_en = pair_sums(slope, normed_in, G)
    grad_in_pre = finish_back(slope, normed_in, inv_in, sum_e, sum_en, members)
    grad_weight_in = correlate(pad_in, grad_in_pre, height, breadth) * factor
    grad_feat = transposed(pad_grid(grad_in_pre), weight_in[:, :, :C], height, breadth)
    grad_features = (cotangent.astype(jnp.float32) + grad_feat).astype(jnp.bfloat16)
    return (output_field, grad_features, grad_weight_in, grad_weight_mid, grad_weight_out)
```

```python
import jax
import jax.numpy as jnp
from jax import lax
from jax.experimental import pallas as pl
from jax.experimental.pallas import tpu as pltpu
from jax.sharding import PartitionSpec as P

C = 128
CC = 40
G = 32
H = 8
W = 256
N = H * W
NP = N + 2 * W
BS = 256
SLOT = 8
NLON = 16
NLAT = 8
CELLS = 64 * 4096
MEMBERS = (C // G) * CELLS
FACTOR = CELLS ** -0.5
EPS = 1e-05
ROWS_IN = 96
ROWS_OM = 144
F32 = jnp.float32
BF16 = jnp.bfloat16
MESH = pl.DeviceIdType.MESH
FEAT, COT, COND, POOL, MERG, GMID, GIN = range(7)
HOPS = (0, 1, 2, 1)
OTHERS = sorted(
    [(a, b, c, d) for a in range(4) for b in range(4) for c in range(4) for d in range(2) if (a, b, c, d) != (0, 0, 0, 0)],
    key=lambda o: -(HOPS[o[0]] + HOPS[o[1]] + HOPS[o[2]]),
)
AROUND = [(a, b) for a in (-1, 0, 1) for b in (-1, 0, 1) if (a, b) != (0, 0)]


def dot(a, b):
    return lax.dot_general(a, b, (((1,), (0,)), ((), ())), preferred_element_type=F32)


def dot_nt(a, b):
    return lax.dot_general(a, b, (((1,), (1,)), ((), ())), preferred_element_type=F32)


def sigmoid(v):
    return 1.0 / (1.0 + jnp.exp(-v))


def kernel(
    feat, cot, blocks, table, src, wt, w_in, w_mid, w_out, gain_in, bias_in, gain_mid, bias_mid,
    out, gfeat, g_in, g_om,
    fc, relay, pool_s, pool_r, onehot, fid, fwt, acc, condf, hidden, gmerged, slope, act, merged, gin, up,
    x3f, x3c, x3m, x3g, x3cond, wf, wc, wo, wm, wt_out, wt_mid, wt_in,
    hr, hc, edge_l, edge_r, chr_, chc, cedge_l, cedge_r, pooled, gmid, near_p, near_g, im_p, im_g,
    a1, gw_in, s_in, s_om, core_in, core_om, half_in, half_om, r1_in, r1_om, r2_in, r2_om, full_in, full_om,
    sem_ps, sem_pr, sem_hs, sem_hr, sem_a, sem_b,
):
    lon = lax.axis_index("lon")
    lat = lax.axis_index("lat")

    def at(dlat, dlon):
        return {"lon": lax.rem(lon + dlon + NLON, NLON), "lat": lat + dlat}

    def has_lat(d):
        if d == 0:
            return None
        return jnp.logical_and(lat + d >= 0, lat + d < NLAT)

    def guarded(cond, fn):
        if cond is None:
            fn()
        else:
            pl.when(cond)(fn)

    finish = []

    def send(cond, source, dest, s_sem, r_sem, device):
        copy = pltpu.make_async_remote_copy(
            src_ref=source, dst_ref=dest, send_sem=s_sem, recv_sem=r_sem,
            device_id=device, device_id_type=MESH,
        )
        guarded(cond, copy.start)
        finish.append((cond, copy.wait_send))

    def arrive(ref, sem):
        pltpu.make_async_copy(ref, ref, sem).wait()

    barrier = pltpu.get_barrier_semaphore()

    core = lax.rem(lon, 2)
    chip = lon // 2
    x = lon // 4
    z = lat // 2
    y = lax.rem(chip, 2) * 2 + lax.rem(lat, 2)
    lon_of = {}
    lat_of = {}
    for oy in range(4):
        y2 = lax.rem(y + oy, 4)
        for oc in range(2):
            for ox in range(4):
                lon_of[ox, oy, oc] = (lax.rem(x + ox, 4) * 2 + y2 // 2) * 2 + (core if oc == 0 else 1 - core)
        for oz in range(4):
            lat_of[oz, oy] = lax.rem(z + oz, 4) * 2 + lax.rem(y2, 2)

    def everyone(act_on):
        for ox, oy, oz, oc in OTHERS:
            act_on({"lon": lon_of[ox, oy, oc], "lat": lat_of[oz, oy]})

    everyone(lambda peer: pl.semaphore_signal(barrier, inc=1, device_id=peer, device_id_type=MESH))

    def relaid(ref, base):
        cells = ref[...].astype(F32).reshape(C * H, W)
        for side in range(2):
            relay[side * C * H:(side + 1) * C * H] = cells[:, side * 128:(side + 1) * 128]
            for r in range(H):
                where = slice(r * W + side * 128, r * W + (side + 1) * 128)
                fc[base:base + C, where] = relay[pl.ds(side * C * H + r, C, stride=H), :].astype(BF16)

    relaid(feat, 0)
    relaid(cot, C)

    gaps = [0, 1, -1, 2, -2, 3, -3, 4, -4]

    def pack(k, dest):
        for s2 in range(0, 4, 2):
            for half in range(2):
                one = jnp.maximum(table[0, lat, lat + gaps[k], 2 * s2 + half], 0)
                two = jnp.maximum(table[0, lat, lat + gaps[k], 2 * s2 + 2 + half], 0)
                both = jnp.concatenate([blocks[0, one].astype(F32), blocks[0, two].astype(F32)], axis=0)
                dest[s2 * CC:(s2 + 2) * CC, half * BS:(half + 1) * BS] = both.astype(BF16)

    pack(0, pool_r.at[0])
    for k in range(1, 9):
        guarded(has_lat(gaps[k]), lambda k=k: pack(k, pool_s.at[k]))

    lane = lax.broadcasted_iota(jnp.int32, (C, 128), 1)

    def edge_columns(ref, offset, chans, left, right):
        lanes = lax.broadcasted_iota(jnp.int32, (chans, 128), 1)
        to_l = jnp.zeros((chans, 128), F32)
        to_r = jnp.zeros((chans, 128), F32)
        for r in range(H):
            base = offset + r * W
            first = ref[:, base:base + 128].astype(F32)
            last = ref[:, base + 128:base + 256].astype(F32)
            to_l = jnp.where(lanes == r + 1, first[:, 0:1], to_l)
            to_r = jnp.where(lanes == r + 1, last[:, 127:128], to_r)
        left[...] = to_l.astype(left.dtype)
        right[...] = to_r.astype(right.dtype)

    edge_columns(fc.at[0:C], 0, C, edge_l.at[FEAT], edge_r.at[FEAT])
    edge_columns(fc.at[C:2 * C], 0, C, edge_l.at[COT], edge_r.at[COT])

    pl.semaphore_wait(barrier, NLAT * NLON - 1)

    def send_fine(f, ref, offset, rows_at, cols_at, left, right):
        send(has_lat(-1), ref.at[:, offset:offset + W], rows_at.at[1], sem_hs.at[f, 0], sem_hr.at[f, 1], at(-1, 0))
        send(has_lat(1), ref.at[:, offset + N - W:offset + N], rows_at.at[0], sem_hs.at[f, 1], sem_hr.at[f, 0], at(1, 0))
        for d in (0, -1, 1):
            send(has_lat(d), right, cols_at.at[1 - d], sem_hs.at[f, 3 + d], sem_hr.at[f, 3 - d], at(d, 1))
            send(has_lat(d), left, cols_at.at[4 - d], sem_hs.at[f, 6 + d], sem_hr.at[f, 6 - d], at(d, -1))

    def expect(cond, ref, sem):
        if cond is None:
            arrive(ref, sem)
            return

        @pl.when(cond)
        def _():
            arrive(ref, sem)

        @pl.when(jnp.logical_not(cond))
        def _():
            ref[...] = jnp.zeros(ref.shape, ref.dtype)

    def wait_fine(f, rows_at, cols_at):
        expect(has_lat(-1), rows_at.at[0], sem_hr.at[f, 0])
        expect(has_lat(1), rows_at.at[1], sem_hr.at[f, 1])
        for d in (0, -1, 1):
            expect(has_lat(d), cols_at.at[1 + d], sem_hr.at[f, 3 + d])
            expect(has_lat(d), cols_at.at[4 + d], sem_hr.at[f, 6 + d])

    for k in range(1, 9):
        back = gaps.index(-gaps[k])
        send(has_lat(gaps[k]), pool_s.at[k], pool_r.at[back], sem_ps.at[k], sem_pr.at[back], at(gaps[k], 0))
    send_fine(FEAT, fc.at[0:C], 0, hr.at[FEAT], hc.at[FEAT], edge_l.at[FEAT], edge_r.at[FEAT])
    send_fine(COT, fc.at[C:2 * C], 0, hr.at[COT], hc.at[COT], edge_l.at[COT], edge_r.at[COT])

    def make_onehot(j, _):
        m = j // H
        r = lax.rem(j, H)
        cells = src[m, pl.ds(r, 1), :]
        low = lax.rem(cells, 2 * BS)
        rows = lax.broadcasted_iota(jnp.int32, (2 * BS, W), 0)
        where = pl.ds(pl.multiple_of(j * W, W), W)
        onehot[:, where] = jnp.where(rows == low, 1.0, 0.0).astype(BF16)
        fid[:, where] = cells // (2 * BS)
        fwt[:, where] = wt[m, pl.ds(r, 1), :]
        return 0

    lax.fori_loop(0, 2 * H, make_onehot, 0)

    for r in range(H):
        small = lax.broadcasted_iota(jnp.int32, (C, W), 0)
        cell = lax.broadcasted_iota(jnp.int32, (C, W), 1)
        up[:, r * W:(r + 1) * W] = jnp.where(small == (r // 4) * 64 + cell // 4, 1.0, 0.0).astype(BF16)

    def turn(t):
        return t.astype(F32).T.astype(BF16)

    for a in range(3):
        rows = []
        for b in range(3):
            t = 3 * a + b
            wf[a, :, b * C:(b + 1) * C] = turn(w_in[t, 0:C, :])
            wo[a, :, b * C:(b + 1) * C] = w_out[t]
            wm[:, t * C:(t + 1) * C] = w_mid[t]
            rows.append(w_in[t, C:C + CC, :].astype(F32))
        wc[a] = jnp.concatenate(rows + [jnp.zeros((8, C), F32)], axis=0).T.astype(BF16)

    def turn_out():
        for t in range(9):
            wt_out[t // 3, :, (t % 3) * C:(t % 3 + 1) * C] = turn(w_out[8 - t])

    def turn_rest():
        for t in range(9):
            wt_mid[:, t * C:(t + 1) * C] = turn(w_mid[8 - t])
            wt_in[t // 3, :, (t % 3) * C:(t % 3 + 1) * C] = w_in[8 - t, 0:C, :]

    def left_right(r, cols_at):
        if r == 0:
            return cols_at[0].astype(F32)[:, 8:9], cols_at[3].astype(F32)[:, 8:9]
        if r == H + 1:
            return cols_at[2].astype(F32)[:, 1:2], cols_at[5].astype(F32)[:, 1:2]
        return cols_at[1].astype(F32)[:, r:r + 1], cols_at[4].astype(F32)[:, r:r + 1]

    def shifted(v, r, cols_at):
        chans = v.shape[0]
        at_lane = lax.broadcasted_iota(jnp.int32, (chans, W), 1)
        first, last = left_right(r, cols_at)
        before = jnp.where(at_lane == 0, first, pltpu.roll(v, 1, 1))
        after = jnp.where(at_lane == W - 1, last, pltpu.roll(v, W - 1, 1))
        return before, after

    def build(x3, ref, rows_at, cols_at):
        for r in range(H + 2):
            if r == 0:
                v = rows_at[0]
            elif r == H + 1:
                v = rows_at[1]
            else:
                v = ref[:, (r - 1) * W:r * W]
            before, after = shifted(v.astype(F32), r, cols_at)
            x3[0:C, r * W:(r + 1) * W] = before.astype(BF16)
            x3[C:2 * C, r * W:(r + 1) * W] = v
            x3[2 * C:3 * C, r * W:(r + 1) * W] = after.astype(BF16)

    STEP = 512

    def conv(weights, x3, use):
        def body(j, _):
            total = None
            for a in range(3):
                start = pl.multiple_of(j * STEP + a * W, W)
                part = dot(weights[a], x3[:, pl.ds(start, STEP)])
                total = part if total is None else total + part
            use(pl.ds(pl.multiple_of(j * STEP, STEP), STEP), total)
            return 0

        lax.fori_loop(0, N // STEP, body, 0)

    def put(ref):
        def use(where, v):
            ref[:, where] = v

        return use

    wait_fine(FEAT, hr.at[FEAT], hc.at[FEAT])
    build(x3f, fc.at[0:C], hr.at[FEAT], hc.at[FEAT])
    conv(wf, x3f, put(hidden))
    turn_out()
    wait_fine(COT, hr.at[COT], hc.at[COT])
    build(x3c, fc.at[C:2 * C], hr.at[COT], hc.at[COT])
    conv(wt_out, x3c, put(gmerged))

    def halves(v):
        high = v.astype(BF16)
        return high, (v - high.astype(F32)).astype(BF16)

    high, low = halves(gmerged[...])
    gsmall = dot_nt(high, up[...]) + dot_nt(low, up[...])

    acc[...] = jnp.zeros(acc.shape, F32)

    def interp(k, _):
        gap = jnp.where(lax.rem(k, 2) == 1, (k + 1) // 2, -(k // 2))
        owner = lat + gap

        @pl.when(jnp.logical_and(owner >= 0, owner < NLAT))
        def _():
            @pl.when(k > 0)
            def _():
                arrive(pool_r.at[k], sem_pr.at[k])

            products = dot(pool_r[k], onehot[...])
            total = acc[...]
            for s2 in range(4):
                mask = jnp.where(fid[...] == owner * 4 + s2, fwt[...], 0.0)
                total = total + products[s2 * CC:(s2 + 1) * CC] * mask
            acc[...] = total

        return 0

    lax.fori_loop(0, 9, interp, 0)

    blended = acc[:, 0:N] + acc[:, N:2 * N]
    condf[:, W:W + N] = blended.astype(BF16).astype(F32)
    edge_columns(condf, W, CC, cedge_l, cedge_r)
    send_fine(COND, condf, W, chr_, chc, cedge_l, cedge_r)
    wait_fine(COND, chr_, chc)
    for r in range(H + 2):
        if r == 0:
            v = chr_[0]
        elif r == H + 1:
            v = chr_[1]
        else:
            v = condf[:, r * W:(r + 1) * W]
        before, after = shifted(v, r, chc)
        stacked = jnp.concatenate([before, v, after, jnp.zeros((8, W), F32)], axis=0)
        x3cond[:, r * W:(r + 1) * W] = stacked.astype(BF16)

    def add_hidden(where, v):
        hidden[:, where] = hidden[:, where] + v

    conv(wc, x3cond, add_hidden)

    chan = lax.broadcasted_iota(jnp.int32, (C, C), 0)
    other = lax.broadcasted_iota(jnp.int32, (C, C), 1)
    eye = chan == other
    to_first = jnp.where(other == chan // (C // G), 1.0, 0.0)
    to_second = jnp.where(other == G + chan // (C // G), 1.0, 0.0)
    me = lat * NLON + lon

    def to_col(row):
        return jnp.sum(jnp.where(eye, row, 0.0), axis=1, keepdims=True)

    def all_sum(k, first, second, beside=None):
        one = jnp.sum(first, axis=1, keepdims=True)
        two = jnp.sum(second, axis=1, keepdims=True)
        mine = a1.at[k, pl.ds(me, 1)]
        a1[k, pl.ds(me, 1), :] = jnp.sum(one * to_first + two * to_second, axis=0, keepdims=True)

        def share(peer):
            pltpu.make_async_remote_copy(
                src_ref=mine, dst_ref=mine, send_sem=sem_a.at[k, 0], recv_sem=sem_a.at[k, 1],
                device_id=peer, device_id_type=MESH,
            ).start()

        everyone(share)
        if beside is not None:
            beside()
        rest = a1.at[k, pl.ds(0, NLAT * NLON - 1)]
        arrive(rest, sem_a.at[k, 1])
        finish.append((None, lambda: arrive(rest, sem_a.at[k, 0])))
        total = jnp.sum(a1[k], axis=0, keepdims=True)
        return (
            jnp.sum(total * to_first, axis=1, keepdims=True),
            jnp.sum(total * to_second, axis=1, keepdims=True),
        )

    def norm_terms(sums, squares, members):
        average = sums / members
        variance = squares / members - average * average
        return average, lax.rsqrt(variance + EPS)

    s = jnp.zeros((C, 128), F32)
    q = jnp.zeros((C, 128), F32)
    for j in range(N // 128):
        v = hidden[:, j * 128:(j + 1) * 128]
        s = s + v
        q = q + v * v
    sums, squares = all_sum(0, s, q, turn_rest)
    avg_in, inv_in = norm_terms(sums, squares, MEMBERS)
    g1 = to_col(gain_in[...])
    b1 = to_col(bias_in[...])
    g2 = to_col(gain_mid[...])
    b2 = to_col(bias_mid[...])

    def activate(j, _):
        where = pl.ds(pl.multiple_of(j * W, W), W)
        affine = g1 * ((hidden[:, where] - avg_in) * inv_in) + b1
        act[:, where] = (affine * sigmoid(affine)).astype(BF16)
        return 0

    lax.fori_loop(0, H, activate, 0)

    def send_coarse(f, ref, near):
        for i, (dlat, dlon) in enumerate(AROUND):
            send(has_lat(dlat), ref, near.at[7 - i], sem_hs.at[f, i], sem_hr.at[f, 7 - i], at(dlat, dlon))

    def wait_coarse(f, near):
        for i, (dlat, dlon) in enumerate(AROUND):
            expect(has_lat(dlat), near.at[i], sem_hr.at[f, i])

    def build_coarse(im, ref, near):
        def column(up_, mid_, down_):
            u, m, d = up_.astype(F32), mid_.astype(F32), down_.astype(F32)
            over = jnp.where(lane < 64, pltpu.roll(u, 64, 1), pltpu.roll(m, 64, 1))
            under = jnp.where(lane < 64, pltpu.roll(m, 64, 1), pltpu.roll(d, 64, 1))
            return over, m, under

        lefts = column(near[0], near[3], near[5])
        mids = column(near[1], ref[...], near[6])
        rights = column(near[2], near[4], near[7])
        for a in range(3):
            before = jnp.where(lane % 64 == 0, pltpu.roll(lefts[a], 65, 1), pltpu.roll(mids[a], 1, 1))
            after = jnp.where(lane % 64 == 63, pltpu.roll(rights[a], 63, 1), pltpu.roll(mids[a], 127, 1))
            im[(3 * a) * C:(3 * a + 1) * C] = before.astype(BF16)
            im[(3 * a + 1) * C:(3 * a + 2) * C] = mids[a].astype(BF16)
            im[(3 * a + 2) * C:(3 * a + 3) * C] = after.astype(BF16)

    pooled[...] = (dot_nt(act[...], up[...]) * (1.0 / 16.0)).astype(BF16)
    send_coarse(POOL, pooled, near_p)
    wait_coarse(POOL, near_p)
    build_coarse(im_p, pooled, near_p)
    hidden_mid = dot(wm[...], im_p[...])
    sums, squares = all_sum(1, hidden_mid, hidden_mid * hidden_mid)
    avg_mid, inv_mid = norm_terms(sums, squares, MEMBERS // 16)
    normed_mid = (hidden_mid - avg_mid) * inv_mid
    affine_mid = g2 * normed_mid + b2
    sig = sigmoid(affine_mid)
    act_mid = (affine_mid * sig).astype(BF16)
    slope_mid = gsmall * sig * (1.0 + affine_mid * (1.0 - sig)) * g2

    def send_merged():
        for r in range(H):
            where = slice(r * W, (r + 1) * W)
            merged[:, where] = (act[:, where].astype(F32) + dot(act_mid, up[:, where])).astype(BF16)
        edge_columns(merged, 0, C, edge_l.at[MERG], edge_r.at[MERG])
        send_fine(MERG, merged, 0, hr.at[MERG], hc.at[MERG], edge_l.at[MERG], edge_r.at[MERG])

    sum_e, sum_en = all_sum(2, slope_mid, slope_mid * normed_mid, send_merged)
    mean_e = sum_e / (MEMBERS // 16)
    mean_en = sum_en / (MEMBERS // 16)
    gmid[...] = ((slope_mid - mean_e - normed_mid * mean_en) * inv_mid).astype(BF16)
    send_coarse(GMID, gmid, near_g)
    g_mid_w = dot_nt(gmid[...], im_p[...])
    for t in range(9):
        s_om[t * C:(t + 1) * C] = g_mid_w[:, t * C:(t + 1) * C].astype(BF16)
    wait_coarse(GMID, near_g)
    build_coarse(im_g, gmid, near_g)
    gpooled = dot(wt_mid[...], im_g[...]) * (1.0 / 16.0)
    high, low = halves(gpooled)

    def slopes(j, carry):
        s, q = carry
        where = pl.ds(pl.multiple_of(j * W, W), W)
        gact = gmerged[:, where] + dot(high, up[:, where]) + dot(low, up[:, where])
        normed = (hidden[:, where] - avg_in) * inv_in
        affine = g1 * normed + b1
        sig = sigmoid(affine)
        e = gact * sig * (1.0 + affine * (1.0 - sig)) * g1
        slope[:, where] = e
        en = e * normed
        return s + e[:, 0:128] + e[:, 128:256], q + en[:, 0:128] + en[:, 128:256]

    s, q = lax.fori_loop(0, H, slopes, (jnp.zeros((C, 128), F32), jnp.zeros((C, 128), F32)))

    jobs = {
        0: (ROWS_OM, s_om, core_om, half_om, r1_om, r2_om, full_om),
        1: (ROWS_IN, s_in, core_in, half_in, r1_in, r2_in, full_in),
    }
    partner = {"lon": lon + 1 - 2 * core, "lat": lat}

    def pieces(ref, n):
        return ref.at[pl.ds(0, n)]

    def hand(k, step, source, dest, peer):
        pltpu.make_async_remote_copy(
            src_ref=source, dst_ref=dest, send_sem=sem_b.at[k, 2 * step], recv_sem=sem_b.at[k, 2 * step + 1],
            device_id=peer, device_id_type=MESH,
        ).start()

    def along_lon(d):
        return lax.rem(chip + d, NLON // 2)

    def cores(k):
        rows, s_ref, got = jobs[k][:3]
        part = pl.ds(pl.multiple_of((1 - core) * 8 * rows, 16), 8 * rows)
        hand(k, 0, s_ref.at[part], got, partner)
        finish.append((None, lambda: arrive(got, sem_b.at[k, 0])))

    def scatter(k):
        rows, s_ref, got, half, r1 = jobs[k][:5]
        arrive(got, sem_b.at[k, 1])
        part = pl.ds(pl.multiple_of(core * 8 * rows, 16), 8 * rows)
        half[...] = (s_ref[part, :].astype(F32) + got[...].astype(F32)).astype(BF16)
        for d in range(1, 8):
            to = along_lon(d)
            hand(k, 1, half.at[pl.ds(pl.multiple_of(to * rows, 16), rows)], r1.at[chip], {"lon": to * 2 + core, "lat": lat})
        r1[chip] = half[pl.ds(pl.multiple_of(chip * rows, 16), rows), :]
        finish.append((None, lambda: arrive(pieces(r1, 7), sem_b.at[k, 2])))

    def added(ref):
        total = ref[0].astype(F32)
        for i in range(1, 8):
            total = total + ref[i].astype(F32)
        return total.astype(BF16)

    def middle(k):
        r1, r2 = jobs[k][4:6]
        arrive(pieces(r1, 7), sem_b.at[k, 3])
        r2[lat] = added(r1)
        for d in range(1, NLAT):
            hand(k, 2, r2.at[lat], r2.at[lat], {"lon": lon, "lat": lax.rem(lat + d, NLAT)})
        finish.append((None, lambda: arrive(pieces(r2, 7), sem_b.at[k, 4])))

    def gather(k):
        r2, full = jobs[k][5:7]
        arrive(pieces(r2, 7), sem_b.at[k, 5])
        full[core, chip] = added(r2)
        for d in range(1, 8):
            hand(k, 3, full.at[core, chip], full.at[core, chip], {"lon": along_lon(d) * 2 + core, "lat": lat})
        finish.append((None, lambda: arrive(pieces(full.at[core], 7), sem_b.at[k, 6])))

    def exchange(k):
        full = jobs[k][6]
        arrive(pieces(full.at[core], 7), sem_b.at[k, 7])
        hand(k, 4, full.at[core], full.at[core], partner)
        finish.append((None, lambda: arrive(full.at[core], sem_b.at[k, 8])))

    def complete(k, result):
        full = jobs[k][6]
        arrive(full.at[1 - core], sem_b.at[k, 9])
        result[...] = full[...]

    def beside_slopes():
        wait_fine(MERG, hr.at[MERG], hc.at[MERG])
        build(x3m, merged, hr.at[MERG], hc.at[MERG])
        for a in range(3):
            part = dot_nt(fc[C:2 * C], x3m[:, a * W:a * W + N])
            for b in range(3):
                t = 9 + 3 * a + b
                s_om[t * C:(t + 1) * C] = part[:, b * C:(b + 1) * C].astype(BF16)
        cores(0)
        scatter(0)

    sum_e, sum_en = all_sum(3, s, q, beside_slopes)
    mean_e = sum_e / MEMBERS
    mean_en = sum_en / MEMBERS

    def finish_in(j, _):
        where = pl.ds(pl.multiple_of(j * W, W), W)
        normed = (hidden[:, where] - avg_in) * inv_in
        gin[:, where] = ((slope[:, where] - mean_e - normed * mean_en) * inv_in).astype(BF16)
        return 0

    lax.fori_loop(0, H, finish_in, 0)

    edge_columns(gin, 0, C, edge_l.at[GIN], edge_r.at[GIN])
    send_fine(GIN, gin, 0, hr.at[GIN], hc.at[GIN], edge_l.at[GIN], edge_r.at[GIN])
    taps = C + CC
    for a in range(3):
        part = dot_nt(x3f[:, a * W:a * W + N], gin[...])
        more = dot_nt(x3cond[:, a * W:a * W + N], gin[...])
        for b in range(3):
            t = 3 * a + b
            gw_in[t * taps:t * taps + C] = part[b * C:(b + 1) * C]
            gw_in[t * taps + C:(t + 1) * taps] = more[b * CC:(b + 1) * CC]
    gw_in[9 * taps:] = jnp.zeros((16 * ROWS_IN - 9 * taps, C), F32)
    s_in[...] = gw_in[...].astype(BF16)
    cores(1)
    middle(0)
    scatter(1)

    def put_out(where, v):
        out[:, where] = (fc[0:C, where].astype(F32) + v).astype(BF16)

    conv(wo, x3m, put_out)
    gather(0)
    middle(1)
    wait_fine(GIN, hr.at[GIN], hc.at[GIN])
    build(x3g, gin, hr.at[GIN], hc.at[GIN])

    def put_feat(where, v):
        gfeat[:, where] = (fc[C:2 * C, where].astype(F32) + v).astype(BF16)

    conv(wt_in, x3g, put_feat)
    gather(1)
    exchange(0)
    complete(0, g_om)
    exchange(1)
    complete(1, g_in)
    for cond, wait in finish:
        guarded(cond, wait)


def local(
    features, coarse_blocks, send_table, interp_src, interp_wt, weight_in, weight_mid, weight_out,
    gain_in, bias_in, gain_mid, bias_mid, cotangent,
):
    vmem = pl.BlockSpec(memory_space=pltpu.VMEM)
    smem = pl.BlockSpec(memory_space=pltpu.SMEM)
    V = pltpu.VMEM
    scratch = [
        V((2 * C, N), BF16), V((2 * C * H, 128), F32),
        V((9, 4 * CC, 2 * BS), BF16), V((9, 4 * CC, 2 * BS), BF16), V((2 * BS, 2 * N), BF16),
        V((1, 2 * N), jnp.int32), V((1, 2 * N), F32),
        V((CC, 2 * N), F32), V((CC, NP), F32), V((C, N), F32), V((C, N), F32), V((C, N), F32),
        V((C, N), BF16), V((C, N), BF16), V((C, N), BF16), V((C, N), BF16),
        V((3 * C, NP), BF16), V((3 * C, NP), BF16), V((3 * C, NP), BF16), V((3 * C, NP), BF16), V((C, NP), BF16),
        V((3, C, 3 * C), BF16), V((3, C, C), BF16), V((3, C, 3 * C), BF16), V((C, 9 * C), BF16),
        V((3, C, 3 * C), BF16), V((C, 9 * C), BF16), V((3, C, 3 * C), BF16),
        V((7, 2, C, W), BF16), V((7, 6, C, 128), BF16), V((7, C, 128), BF16), V((7, C, 128), BF16),
        V((2, CC, W), F32), V((6, CC, 128), F32), V((CC, 128), F32), V((CC, 128), F32),
        V((C, 128), BF16), V((C, 128), BF16), V((8, C, 128), BF16), V((8, C, 128), BF16),
        V((9 * C, 128), BF16), V((9 * C, 128), BF16),
        V((4, NLAT * NLON, C), F32), V((16 * ROWS_IN, C), F32),
        V((16 * ROWS_IN, C), BF16), V((16 * ROWS_OM, C), BF16), V((8 * ROWS_IN, C), BF16), V((8 * ROWS_OM, C), BF16),
        V((8 * ROWS_IN, C), BF16), V((8 * ROWS_OM, C), BF16), V((8, ROWS_IN, C), BF16), V((8, ROWS_OM, C), BF16),
        V((8, ROWS_IN, C), BF16), V((8, ROWS_OM, C), BF16), V((2, 8, ROWS_IN, C), BF16), V((2, 8, ROWS_OM, C), BF16),
        pltpu.SemaphoreType.DMA((9,)), pltpu.SemaphoreType.DMA((9,)),
        pltpu.SemaphoreType.DMA((7, 8)), pltpu.SemaphoreType.DMA((7, 8)),
        pltpu.SemaphoreType.DMA((4, 2)), pltpu.SemaphoreType.DMA((2, 10)),
    ]
    out, gfeat, g_in, g_om = pl.pallas_call(
        kernel,
        out_shape=(
            jax.ShapeDtypeStruct((C, N), BF16), jax.ShapeDtypeStruct((C, N), BF16),
            jax.ShapeDtypeStruct((2, 8, ROWS_IN, C), BF16), jax.ShapeDtypeStruct((2, 8, ROWS_OM, C), BF16),
        ),
        in_specs=[vmem, vmem, vmem, smem] + [vmem] * 9,
        out_specs=(vmem,) * 4,
        scratch_shapes=scratch,
        compiler_params=pltpu.CompilerParams(
            collective_id=0, has_side_effects=True, vmem_limit_bytes=56 * 1024 * 1024
        ),
    )(
        features, cotangent, coarse_blocks, send_table, interp_src, interp_wt, jnp.swapaxes(weight_in, 1, 2), weight_mid, weight_out,
        gain_in.reshape(1, C), bias_in.reshape(1, C), gain_mid.reshape(1, C), bias_mid.reshape(1, C),
    )
    shape = features.shape
    grad_in = g_in.reshape(16 * ROWS_IN, C)[:9 * (C + CC)].reshape(9, C + CC, C).astype(F32) * FACTOR
    grad_in = jnp.swapaxes(grad_in, 1, 2)
    taps = g_om.reshape(18, C, C)
    grad_mid = taps[:9].astype(F32) * FACTOR
    grad_out = taps[9:].astype(F32) * FACTOR
    return out.reshape(shape), gfeat.reshape(shape), grad_in, grad_mid, grad_out


def solution(mesh):
    tile = P(None, "lat", "lon")
    in_specs = (
        tile, P("lon", "lat", None, None), P("lon", None, None, None), tile, tile,
        P(), P(), P(), P(), P(), P(), P(), tile,
    )
    out_specs = (tile, tile, P(), P(), P())
    return jax.shard_map(local, mesh=mesh, in_specs=in_specs, out_specs=out_specs, check_vma=False)
```

```python
import jax
import jax.numpy as jnp
from jax import lax
from jax.experimental import pallas as pl
from jax.experimental.pallas import tpu as pltpu
from jax.sharding import PartitionSpec as P

C = 128
CC = 40
G = 32
H = 8
W = 256
N = H * W
NP = N + 2 * W
BS = 256
SLOT = 8
NLON = 16
NLAT = 8
CELLS = 64 * 4096
MEMBERS = (C // G) * CELLS
FACTOR = CELLS ** -0.5
EPS = 1e-05
ROWS_IN = 96
ROWS_OM = 144
AT_OM = 4 * H * C
AT_IN = AT_OM + 16 * ROWS_OM
ROWS = AT_IN + 16 * ROWS_IN
F32 = jnp.float32
BF16 = jnp.bfloat16
MESH = pl.DeviceIdType.MESH
FEAT, COT, COND, POOL, MERG, GMID, GIN = range(7)
HOPS = (0, 1, 2, 1)
OTHERS = sorted(
    [(a, b, c, d) for a in range(4) for b in range(4) for c in range(4) for d in range(2) if (a, b, c, d) != (0, 0, 0, 0)],
    key=lambda o: -(HOPS[o[0]] + HOPS[o[1]] + HOPS[o[2]]),
)


def dot(a, b):
    return lax.dot_general(a, b, (((1,), (0,)), ((), ())), preferred_element_type=F32)


def dot_nt(a, b):
    return lax.dot_general(a, b, (((1,), (1,)), ((), ())), preferred_element_type=F32)


def sigmoid(v):
    return 1.0 / (1.0 + jnp.exp(-v))


def kernel(
    feat, cot, blocks, table, src, wt, w_in, w_mid, w_out, gain_in, bias_in, gain_mid, bias_mid,
    res,
    fc, relay, pool_s, pool_r, onehot, fid, fwt, acc, condf, hidden, gmerged, slope, act, merged, gin, up,
    x3f, x3c, x3m, x3g, x3cond, wf, wc, wo, wm, wt_out, wt_mid, wt_in,
    hr, hc, edge, crow, chr_, pooled, pooled_e, gmid, slope_r, slope_e, row_p, pack_p, row_g, pack_g, im_p, im_g,
    a1, gw_in, s_in, s_om, core_in, core_om, half_in, half_om, r1_in, r1_om, r2_in, r2_om, full_in, full_om,
    sem_ps, sem_pr, sem_hs, sem_hr, sem_a, sem_b,
):
    lon = lax.axis_index("lon")
    lat = lax.axis_index("lat")

    def at(dlat, dlon):
        return {"lon": lax.rem(lon + dlon + NLON, NLON), "lat": lat + dlat}

    def has_lat(d):
        if d == 0:
            return None
        return jnp.logical_and(lat + d >= 0, lat + d < NLAT)

    def guarded(cond, fn):
        if cond is None:
            fn()
        else:
            pl.when(cond)(fn)

    finish = []

    def send(cond, source, dest, s_sem, r_sem, device):
        copy = pltpu.make_async_remote_copy(
            src_ref=source, dst_ref=dest, send_sem=s_sem, recv_sem=r_sem,
            device_id=device, device_id_type=MESH,
        )
        guarded(cond, copy.start)
        finish.append((cond, copy.wait_send))

    def arrive(ref, sem):
        pltpu.make_async_copy(ref, ref, sem).wait()

    barrier = pltpu.get_barrier_semaphore()

    core = lax.rem(lon, 2)
    chip = lon // 2
    x = lon // 4
    z = lat // 2
    y = lax.rem(chip, 2) * 2 + lax.rem(lat, 2)
    lon_of = {}
    lat_of = {}
    for oy in range(4):
        y2 = lax.rem(y + oy, 4)
        for oc in range(2):
            for ox in range(4):
                lon_of[ox, oy, oc] = (lax.rem(x + ox, 4) * 2 + y2 // 2) * 2 + (core if oc == 0 else 1 - core)
        for oz in range(4):
            lat_of[oz, oy] = lax.rem(z + oz, 4) * 2 + lax.rem(y2, 2)

    def everyone(act_on):
        for ox, oy, oz, oc in OTHERS:
            act_on({"lon": lon_of[ox, oy, oc], "lat": lat_of[oz, oy]})

    everyone(lambda peer: pl.semaphore_signal(barrier, inc=1, device_id=peer, device_id_type=MESH))

    def relaid(ref, base):
        cells = ref[...].astype(F32).reshape(C * H, W)
        for side in range(2):
            relay[side * C * H:(side + 1) * C * H] = cells[:, side * 128:(side + 1) * 128]
            for r in range(H):
                where = slice(r * W + side * 128, r * W + (side + 1) * 128)
                fc[base:base + C, where] = relay[pl.ds(side * C * H + r, C, stride=H), :].astype(BF16)

    relaid(feat, 0)
    relaid(cot, C)

    gaps = [0, 2, -2, 4, -4, 1, -1, 3, -3]

    def pack(k, dest):
        for s2 in range(0, 4, 2):
            for half in range(2):
                one = jnp.maximum(table[0, lat, lat + gaps[k], 2 * s2 + half], 0)
                two = jnp.maximum(table[0, lat, lat + gaps[k], 2 * s2 + 2 + half], 0)
                both = jnp.concatenate([blocks[0, one].astype(F32), blocks[0, two].astype(F32)], axis=0)
                dest[s2 * CC:(s2 + 2) * CC, half * BS:(half + 1) * BS] = both.astype(BF16)

    pack(0, pool_r.at[0])
    for k in range(1, 9):
        guarded(has_lat(gaps[k]), lambda k=k: pack(k, pool_s.at[k]))

    def edge_columns(ref, offset, chans, to):
        lanes = lax.broadcasted_iota(jnp.int32, (chans, 128), 1)
        tile = jnp.zeros((chans, 128), F32)
        for r in range(H):
            base = offset + r * W
            first = ref[:, base:base + 128].astype(F32)
            last = ref[:, base + 128:base + 256].astype(F32)
            tile = jnp.where(lanes == r + 1, first[:, 0:1], tile)
            tile = jnp.where(lanes == r + 17, last[:, 127:128], tile)
        if chans < C:
            tile = jnp.concatenate([tile, jnp.zeros((C - chans, 128), F32)], axis=0)
        to[...] = tile.T[0:32].astype(BF16)

    edge_columns(fc.at[0:C], 0, C, edge.at[FEAT])
    edge_columns(fc.at[C:2 * C], 0, C, edge.at[COT])

    def make_onehot(j, _):
        m = j // H
        r = lax.rem(j, H)
        cells = src[m, pl.ds(r, 1), :]
        low = lax.rem(cells, 2 * BS)
        rows = lax.broadcasted_iota(jnp.int32, (2 * BS, W), 0)
        where = pl.ds(pl.multiple_of(j * W, W), W)
        onehot[:, where] = jnp.where(rows == low, 1.0, 0.0).astype(BF16)
        fid[:, where] = cells // (2 * BS)
        fwt[:, where] = wt[m, pl.ds(r, 1), :]
        return 0

    lax.fori_loop(0, 2 * H, make_onehot, 0)

    for r in range(H):
        small = lax.broadcasted_iota(jnp.int32, (C, W), 0)
        cell = lax.broadcasted_iota(jnp.int32, (C, W), 1)
        up[:, r * W:(r + 1) * W] = jnp.where(small == (r // 4) * 64 + cell // 4, 1.0, 0.0).astype(BF16)

    def turn(t):
        return t.astype(F32).T.astype(BF16)

    for a in range(3):
        rows = []
        for b in range(3):
            t = 3 * a + b
            wf[a, :, b * C:(b + 1) * C] = turn(w_in[t, 0:C, :])
            wo[a, :, b * C:(b + 1) * C] = w_out[t]
            wm[:, t * C:(t + 1) * C] = w_mid[t]
            rows.append(w_in[t, C:C + CC, :].astype(F32))
        wc[a] = jnp.concatenate(rows + [jnp.zeros((8, C), F32)], axis=0).T.astype(BF16)

    def turn_out():
        for t in range(9):
            wt_out[t // 3, :, (t % 3) * C:(t % 3 + 1) * C] = turn(w_out[8 - t])

    def turn_rest():
        for t in range(9):
            wt_mid[:, t * C:(t + 1) * C] = turn(w_mid[8 - t])
            wt_in[t // 3, :, (t % 3) * C:(t % 3 + 1) * C] = w_in[8 - t, 0:C, :]

    turn_out()

    pl.semaphore_wait(barrier, NLAT * NLON - 1)

    def send_fine(f, up_row, down_row, rows_at):
        send(has_lat(-1), up_row, rows_at.at[1], sem_hs.at[f, 0], sem_hr.at[f, 1], at(-1, 0))
        send(has_lat(1), down_row, rows_at.at[0], sem_hs.at[f, 1], sem_hr.at[f, 0], at(1, 0))
        for d in (0, -1, 1):
            left, right = edge.at[f, pl.ds(0, 16)], edge.at[f, pl.ds(16, 16)]
            send(has_lat(d), right, hc.at[f, pl.ds(16 - 16 * d, 16)], sem_hs.at[f, 3 + d], sem_hr.at[f, 3 - d], at(d, 1))
            send(has_lat(d), left, hc.at[f, pl.ds(64 - 16 * d, 16)], sem_hs.at[f, 6 + d], sem_hr.at[f, 6 - d], at(d, -1))

    def send_field(f, ref):
        send_fine(f, ref.at[:, 0:W], ref.at[:, N - W:N], hr.at[f])

    def expect(cond, ref, sem):
        if cond is None:
            arrive(ref, sem)
            return

        @pl.when(cond)
        def _():
            arrive(ref, sem)

        @pl.when(jnp.logical_not(cond))
        def _():
            ref[...] = jnp.zeros(ref.shape, ref.dtype)

    def wait_fine(f, rows_at):
        expect(has_lat(-1), rows_at.at[0], sem_hr.at[f, 0])
        expect(has_lat(1), rows_at.at[1], sem_hr.at[f, 1])
        for d in (0, -1, 1):
            expect(has_lat(d), hc.at[f, pl.ds(16 + 16 * d, 16)], sem_hr.at[f, 3 + d])
            expect(has_lat(d), hc.at[f, pl.ds(64 + 16 * d, 16)], sem_hr.at[f, 6 + d])
        cols = hc[f, 0:96, :].astype(F32)
        return jnp.concatenate([cols, jnp.zeros((32, C), F32)], axis=0).T

    def pool_copy(k):
        back = gaps.index(-gaps[k])
        return pltpu.make_async_remote_copy(
            src_ref=pool_s.at[k], dst_ref=pool_r.at[back], send_sem=sem_ps.at[k], recv_sem=sem_pr.at[back],
            device_id=at(gaps[k], 0), device_id_type=MESH,
        )

    for k in (5, 6, 7, 8, 1, 2, 3, 4):
        copy = pool_copy(k)
        guarded(has_lat(gaps[k]), copy.start)
        finish.append((has_lat(gaps[k]), copy.wait_send))
    send_field(FEAT, fc.at[0:C])
    send_field(COT, fc.at[C:2 * C])

    def left_right(r, cols):
        if r == 0:
            return cols[:, 8:9], cols[:, 56:57]
        if r == H + 1:
            return cols[:, 33:34], cols[:, 81:82]
        return cols[:, 16 + r:17 + r], cols[:, 64 + r:65 + r]

    def shifted(v, r, cols):
        chans = v.shape[0]
        at_lane = lax.broadcasted_iota(jnp.int32, (chans, W), 1)
        first, last = left_right(r, cols)
        before = jnp.where(at_lane == 0, first, pltpu.roll(v, 1, 1))
        after = jnp.where(at_lane == W - 1, last, pltpu.roll(v, W - 1, 1))
        return before, after

    def build(x3, ref, rows_at, cols):
        for r in range(H + 2):
            if r == 0:
                v = rows_at[0]
            elif r == H + 1:
                v = rows_at[1]
            else:
                v = ref[:, (r - 1) * W:r * W]
            before, after = shifted(v.astype(F32), r, cols)
            x3[0:C, r * W:(r + 1) * W] = before.astype(BF16)
            x3[C:2 * C, r * W:(r + 1) * W] = v
            x3[2 * C:3 * C, r * W:(r + 1) * W] = after.astype(BF16)

    STEP = 512

    def conv(weights, x3, use):
        def body(j, _):
            total = None
            for a in range(3):
                start = pl.multiple_of(j * STEP + a * W, W)
                part = dot(weights[a], x3[:, pl.ds(start, STEP)])
                total = part if total is None else total + part
            use(pl.ds(pl.multiple_of(j * STEP, STEP), STEP), total)
            return 0

        lax.fori_loop(0, N // STEP, body, 0)

    def put(ref):
        def use(where, v):
            ref[:, where] = v

        return use

    build(x3f, fc.at[0:C], hr.at[FEAT], wait_fine(FEAT, hr.at[FEAT]))
    conv(wf, x3f, put(hidden))
    build(x3c, fc.at[C:2 * C], hr.at[COT], wait_fine(COT, hr.at[COT]))
    conv(wt_out, x3c, put(gmerged))

    def halves(v):
        high = v.astype(BF16)
        return high, (v - high.astype(F32)).astype(BF16)

    high, low = halves(gmerged[...])
    gsmall = dot_nt(high, up[...]) + dot_nt(low, up[...])

    acc[...] = jnp.zeros(acc.shape, F32)

    def interp(k, _):
        size = lax.rem(2 * ((k + 1) // 2), 5)
        gap = jnp.where(lax.rem(k, 2) == 1, size, -size)
        owner = lat + gap

        @pl.when(jnp.logical_and(owner >= 0, owner < NLAT))
        def _():
            @pl.when(k > 0)
            def _():
                arrive(pool_r.at[k], sem_pr.at[k])

            products = dot(pool_r[k], onehot[...])
            total = acc[...]
            for s2 in range(4):
                mask = jnp.where(fid[...] == owner * 4 + s2, fwt[...], 0.0)
                total = total + products[s2 * CC:(s2 + 1) * CC] * mask
            acc[...] = total

        return 0

    lax.fori_loop(0, 9, interp, 0)

    blended = acc[:, 0:N] + acc[:, N:2 * N]
    condf[:, W:W + N] = blended.astype(BF16).astype(F32)
    edge_columns(condf, W, CC, edge.at[COND])
    for i, start in enumerate((W, N)):
        row = jnp.concatenate([condf[:, start:start + W], jnp.zeros((8, W), F32)], axis=0)
        crow[i] = row.astype(BF16)
    send_fine(COND, crow.at[0], crow.at[1], chr_)
    cond_cols = wait_fine(COND, chr_)[0:CC]
    for r in range(H + 2):
        if r == 0:
            v = chr_[0].astype(F32)[0:CC]
        elif r == H + 1:
            v = chr_[1].astype(F32)[0:CC]
        else:
            v = condf[:, r * W:(r + 1) * W]
        before, after = shifted(v, r, cond_cols)
        stacked = jnp.concatenate([before, v, after, jnp.zeros((8, W), F32)], axis=0)
        x3cond[:, r * W:(r + 1) * W] = stacked.astype(BF16)

    def add_hidden(where, v):
        hidden[:, where] = hidden[:, where] + v

    conv(wc, x3cond, add_hidden)

    chan = lax.broadcasted_iota(jnp.int32, (C, C), 0)
    other = lax.broadcasted_iota(jnp.int32, (C, C), 1)
    eye = chan == other
    to_first = jnp.where(other == chan // (C // G), 1.0, 0.0)
    to_second = jnp.where(other == G + chan // (C // G), 1.0, 0.0)
    me = lat * NLON + lon

    def to_row(col):
        return jnp.sum(jnp.where(eye, col, 0.0), axis=0, keepdims=True)

    def to_col(row):
        return jnp.sum(jnp.where(eye, row, 0.0), axis=1, keepdims=True)

    def all_sum(k, first, second, beside=None):
        one = jnp.sum(first, axis=1, keepdims=True)
        two = jnp.sum(second, axis=1, keepdims=True)
        mine = a1.at[k, pl.ds(me, 1)]
        a1[k, pl.ds(me, 1), :] = jnp.sum(one * to_first + two * to_second, axis=0, keepdims=True)

        def share(peer):
            pltpu.make_async_remote_copy(
                src_ref=mine, dst_ref=mine, send_sem=sem_a.at[k, 0], recv_sem=sem_a.at[k, 1],
                device_id=peer, device_id_type=MESH,
            ).start()

        everyone(share)
        if beside is not None:
            beside()
        rest = a1.at[k, pl.ds(0, NLAT * NLON - 1)]
        arrive(rest, sem_a.at[k, 1])
        finish.append((None, lambda: arrive(rest, sem_a.at[k, 0])))
        total = jnp.sum(a1[k], axis=0, keepdims=True)
        return (
            jnp.sum(total * to_first, axis=1, keepdims=True),
            jnp.sum(total * to_second, axis=1, keepdims=True),
        )

    def norm_terms(sums, squares, members):
        average = sums / members
        variance = squares / members - average * average
        return average, lax.rsqrt(variance + EPS)

    s = jnp.zeros((C, 128), F32)
    q = jnp.zeros((C, 128), F32)
    for j in range(N // 128):
        v = hidden[:, j * 128:(j + 1) * 128]
        s = s + v
        q = q + v * v
    sums, squares = all_sum(0, s, q, turn_rest)
    avg_in, inv_in = norm_terms(sums, squares, MEMBERS)
    g1 = to_col(gain_in[...])
    b1 = to_col(bias_in[...])
    g2 = to_col(gain_mid[...])
    b2 = to_col(bias_mid[...])

    def activate(j, _):
        where = pl.ds(pl.multiple_of(j * W, W), W)
        affine = g1 * ((hidden[:, where] - avg_in) * inv_in) + b1
        act[:, where] = (affine * sigmoid(affine)).astype(BF16)
        return 0

    lax.fori_loop(0, H, activate, 0)

    def send_coarse(f, rows, near, mine, packs):
        half = rows.shape[0] // 2
        send(has_lat(-1), rows.at[pl.ds(0, half)], near.at[1], sem_hs.at[f, 0], sem_hr.at[f, 1], at(-1, 0))
        send(has_lat(1), rows.at[pl.ds(half, half)], near.at[0], sem_hs.at[f, 1], sem_hr.at[f, 0], at(1, 0))
        for d in (0, -1, 1):
            send(has_lat(d), mine, packs.at[1 - d], sem_hs.at[f, 3 + d], sem_hr.at[f, 3 - d], at(d, 1))
            send(has_lat(d), mine, packs.at[4 - d], sem_hs.at[f, 6 + d], sem_hr.at[f, 6 - d], at(d, -1))

    def wait_coarse(f, near, packs):
        expect(has_lat(-1), near.at[0], sem_hr.at[f, 0])
        expect(has_lat(1), near.at[1], sem_hr.at[f, 1])
        for d in (0, -1, 1):
            expect(has_lat(d), packs.at[1 + d], sem_hr.at[f, 3 + d])
            expect(has_lat(d), packs.at[4 + d], sem_hr.at[f, 6 + d])

    sub16 = lax.broadcasted_iota(jnp.int32, (16, C), 0)

    def corner_rows(v, first, base):
        for i, n in enumerate((0, 64, 63, 127)):
            base = jnp.where(sub16 == first + i, v[n:n + 1], base)
        return base

    def around(own, near, packs, part, first):
        size = 64
        above = near[0].astype(F32)[part * size:(part + 1) * size]
        below = near[1].astype(F32)[part * size:(part + 1) * size]
        full = jnp.concatenate([above, own, below], axis=0)
        ends = [packs[i].astype(F32) for i in range(6)]

        def row(i, n):
            return ends[i][first + n:first + n + 1]

        lefts = [row(0, 3), row(1, 2), row(1, 3), row(2, 2)]
        rights = [row(3, 1), row(4, 0), row(4, 1), row(5, 0)]
        return full, lefts, rights

    cells = lax.broadcasted_iota(jnp.int32, (2 * C, C), 0)

    def build_coarse(im, full, lefts, rights):
        before = pltpu.roll(full, 1, 0)
        after = pltpu.roll(full, 2 * C - 1, 0)
        for k in range(4):
            before = jnp.where(cells == 64 * k, lefts[k], before)
            after = jnp.where(cells == 64 * k + 63, rights[k], after)
        for b, v in enumerate((before, full, after)):
            v = v.astype(BF16)
            for a in range(3):
                im[:, (3 * a + b) * C:(3 * a + b + 1) * C] = v[a * 64:a * 64 + C]

    own = (dot_nt(up[...], act[...]) * (1.0 / 16.0)).astype(BF16)
    pooled[...] = own
    own = own.astype(F32)
    pooled_e[...] = corner_rows(own, 0, jnp.zeros((16, C), F32)).astype(BF16)
    send_coarse(POOL, pooled, row_p, pooled_e, pack_p)
    wait_coarse(POOL, row_p, pack_p)
    build_coarse(im_p, *around(own, row_p, pack_p, 0, 0))
    hidden_mid = dot_nt(wm[...], im_p[...])
    sums, squares = all_sum(1, hidden_mid, hidden_mid * hidden_mid)
    avg_mid, inv_mid = norm_terms(sums, squares, MEMBERS // 16)
    normed_mid = (hidden_mid - avg_mid) * inv_mid
    affine_mid = g2 * normed_mid + b2
    sig = sigmoid(affine_mid)
    act_mid = (affine_mid * sig).astype(BF16)
    slope_mid = gsmall * sig * (1.0 + affine_mid * (1.0 - sig)) * g2
    slope_t = slope_mid.T
    normed_t = normed_mid.T

    def send_slopes():
        for i, n in enumerate((0, 64)):
            slope_r[i * C:i * C + 64] = slope_t[n:n + 64].astype(BF16)
            slope_r[i * C + 64:(i + 1) * C] = normed_t[n:n + 64].astype(BF16)
        ends = corner_rows(slope_t, 0, jnp.zeros((16, C), F32))
        slope_e[...] = corner_rows(normed_t, 4, ends).astype(BF16)
        send_coarse(GMID, slope_r, row_g, slope_e, pack_g)
        for r in range(H):
            where = slice(r * W, (r + 1) * W)
            merged[:, where] = (act[:, where].astype(F32) + dot(act_mid, up[:, where])).astype(BF16)
        edge_columns(merged, 0, C, edge.at[MERG])
        send_field(MERG, merged)

    sum_e, sum_en = all_sum(2, slope_mid, slope_mid * normed_mid, send_slopes)
    mean_e = sum_e / (MEMBERS // 16)
    mean_en = sum_en / (MEMBERS // 16)
    gmid[...] = ((slope_mid - mean_e - normed_mid * mean_en) * inv_mid).astype(BF16)
    wait_coarse(GMID, row_g, pack_g)
    row_e, row_en, row_inv = to_row(mean_e), to_row(mean_en), to_row(inv_mid)
    inside = [jnp.where(lat > 0, 1.0, 0.0), 1.0, 1.0, jnp.where(lat < NLAT - 1, 1.0, 0.0)]

    def settled(e, normed):
        return (e - row_e - normed * row_en) * row_inv

    e_all, e_left, e_right = around(slope_t, row_g, pack_g, 0, 0)
    n_all, n_left, n_right = around(normed_t, row_g, pack_g, 1, 4)
    valid = jnp.where(cells < 64, inside[0], jnp.where(cells < 192, 1.0, inside[3]))
    build_coarse(
        im_g,
        settled(e_all, n_all) * valid,
        [settled(e_left[k], n_left[k]) * inside[k] for k in range(4)],
        [settled(e_right[k], n_right[k]) * inside[k] for k in range(4)],
    )
    gpooled = dot_nt(wt_mid[...], im_g[...]) * (1.0 / 16.0)
    high, low = halves(gpooled)

    def slopes(j, carry):
        s, q = carry
        where = pl.ds(pl.multiple_of(j * W, W), W)
        gact = gmerged[:, where] + dot(high, up[:, where]) + dot(low, up[:, where])
        normed = (hidden[:, where] - avg_in) * inv_in
        affine = g1 * normed + b1
        sig = sigmoid(affine)
        e = gact * sig * (1.0 + affine * (1.0 - sig)) * g1
        slope[:, where] = e
        en = e * normed
        return s + e[:, 0:128] + e[:, 128:256], q + en[:, 0:128] + en[:, 128:256]

    s, q = lax.fori_loop(0, H, slopes, (jnp.zeros((C, 128), F32), jnp.zeros((C, 128), F32)))

    jobs = {
        0: (ROWS_OM, s_om, core_om, half_om, r1_om, r2_om, full_om),
        1: (ROWS_IN, s_in, core_in, half_in, r1_in, r2_in, full_in),
    }
    partner = {"lon": lon + 1 - 2 * core, "lat": lat}

    def pieces(ref, n):
        return ref.at[pl.ds(0, n)]

    def hand(k, step, source, dest, peer):
        pltpu.make_async_remote_copy(
            src_ref=source, dst_ref=dest, send_sem=sem_b.at[k, 2 * step], recv_sem=sem_b.at[k, 2 * step + 1],
            device_id=peer, device_id_type=MESH,
        ).start()

    def along_lon(d):
        return lax.rem(chip + d, NLON // 2)

    def cores(k):
        rows, s_ref, got = jobs[k][:3]
        part = pl.ds(pl.multiple_of((1 - core) * 8 * rows, 16), 8 * rows)
        hand(k, 0, s_ref.at[part], got, partner)
        finish.append((None, lambda: arrive(got, sem_b.at[k, 0])))

    def scatter(k):
        rows, s_ref, got, half, r1 = jobs[k][:5]
        arrive(got, sem_b.at[k, 1])
        part = pl.ds(pl.multiple_of(core * 8 * rows, 16), 8 * rows)
        half[...] = (s_ref[part, :].astype(F32) + got[...].astype(F32)).astype(BF16)
        for d in range(1, 8):
            to = along_lon(d)
            hand(k, 1, half.at[pl.ds(pl.multiple_of(to * rows, 16), rows)], r1.at[chip], {"lon": to * 2 + core, "lat": lat})
        r1[chip] = half[pl.ds(pl.multiple_of(chip * rows, 16), rows), :]
        finish.append((None, lambda: arrive(pieces(r1, 7), sem_b.at[k, 2])))

    def added(ref):
        total = ref[0].astype(F32)
        for i in range(1, 8):
            total = total + ref[i].astype(F32)
        return total.astype(BF16)

    def middle(k):
        r1, r2 = jobs[k][4:6]
        arrive(pieces(r1, 7), sem_b.at[k, 3])
        r2[lat] = added(r1)
        for d in range(1, NLAT):
            hand(k, 2, r2.at[lat], r2.at[lat], {"lon": lon, "lat": lax.rem(lat + d, NLAT)})
        finish.append((None, lambda: arrive(pieces(r2, 7), sem_b.at[k, 4])))

    def gather(k):
        r2, full = jobs[k][5:7]
        arrive(pieces(r2, 7), sem_b.at[k, 5])
        full[core, chip] = added(r2)
        for d in range(1, 8):
            hand(k, 3, full.at[core, chip], full.at[core, chip], {"lon": along_lon(d) * 2 + core, "lat": lat})
        finish.append((None, lambda: arrive(pieces(full.at[core], 7), sem_b.at[k, 6])))

    def exchange(k):
        full = jobs[k][6]
        arrive(pieces(full.at[core], 7), sem_b.at[k, 7])
        hand(k, 4, full.at[core], full.at[core], partner)
        finish.append((None, lambda: arrive(full.at[core], sem_b.at[k, 8])))

    def complete(k, base):
        rows, full = jobs[k][0], jobs[k][6]
        arrive(full.at[1 - core], sem_b.at[k, 9])
        res[base:base + 16 * rows] = full[...].reshape(16 * rows, C)

    def beside_slopes():
        build(x3m, merged, hr.at[MERG], wait_fine(MERG, hr.at[MERG]))
        for a in range(3):
            part = dot_nt(fc[C:2 * C], x3m[:, a * W:a * W + N])
            for b in range(3):
                t = 9 + 3 * a + b
                s_om[t * C:(t + 1) * C] = part[:, b * C:(b + 1) * C].astype(BF16)
        g_mid_w = dot(gmid[...], im_p[...])
        for t in range(9):
            s_om[t * C:(t + 1) * C] = g_mid_w[:, t * C:(t + 1) * C].astype(BF16)
        cores(0)

    sum_e, sum_en = all_sum(3, s, q, beside_slopes)
    scatter(0)
    mean_e = sum_e / MEMBERS
    mean_en = sum_en / MEMBERS

    def finish_in(j, _):
        where = pl.ds(pl.multiple_of(j * W, W), W)
        normed = (hidden[:, where] - avg_in) * inv_in
        gin[:, where] = ((slope[:, where] - mean_e - normed * mean_en) * inv_in).astype(BF16)
        return 0

    lax.fori_loop(0, H, finish_in, 0)

    taps = C + CC
    for a in range(3):
        part = dot_nt(x3f[:, a * W:a * W + N], gin[...])
        more = dot_nt(x3cond[:, a * W:a * W + N], gin[...])
        for b in range(3):
            t = 3 * a + b
            gw_in[t * taps:t * taps + C] = part[b * C:(b + 1) * C]
            gw_in[t * taps + C:(t + 1) * taps] = more[b * CC:(b + 1) * CC]
    gw_in[9 * taps:] = jnp.zeros((16 * ROWS_IN - 9 * taps, C), F32)
    s_in[...] = gw_in[...].astype(BF16)
    cores(1)
    edge_columns(gin, 0, C, edge.at[GIN])
    send_field(GIN, gin)
    scatter(1)

    def put_rows(base, where, v):
        for i in range(STEP // 128):
            res[pl.ds(pl.multiple_of(base + where.start + i * 128, 128), C)] = v[:, i * 128:(i + 1) * 128]

    def put_out(where, v):
        put_rows(0, where, (fc[0:C, where].astype(F32) + v).astype(BF16))

    conv(wo, x3m, put_out)
    middle(0)
    middle(1)
    build(x3g, gin, hr.at[GIN], wait_fine(GIN, hr.at[GIN]))

    def put_feat(where, v):
        put_rows(2 * H * C, where, (fc[C:2 * C, where].astype(F32) + v).astype(BF16))

    gather(0)
    conv(wt_in, x3g, put_feat)
    gather(1)
    exchange(0)
    complete(0, AT_OM)
    exchange(1)
    complete(1, AT_IN)
    for cond, wait in finish:
        guarded(cond, wait)


def results(res_h, field, features, grad_in, grad_mid, grad_out, res, relay, sem):
    move = pltpu.make_async_copy(res_h, res, sem)
    move.start()
    move.wait()
    for base, dest in ((0, field), (2 * H * C, features)):
        for side in range(2):
            for r in range(H):
                start = base + (2 * r + side) * C
                relay[pl.ds(r, C, stride=H), :] = res[start:start + C].astype(F32)
            dest[:, :, side * 128:(side + 1) * 128] = relay[...].reshape(C, H, 128).astype(BF16)
    for t in range(9):
        rows = slice(AT_IN + t * (C + CC), AT_IN + (t + 1) * (C + CC))
        grad_in[t] = res[rows].astype(F32) * FACTOR
        grad_mid[t] = res[AT_OM + t * C:AT_OM + (t + 1) * C].astype(F32) * FACTOR
        grad_out[t] = res[AT_OM + (9 + t) * C:AT_OM + (10 + t) * C].astype(F32) * FACTOR


def local(
    features, coarse_blocks, send_table, interp_src, interp_wt, weight_in, weight_mid, weight_out,
    gain_in, bias_in, gain_mid, bias_mid, cotangent,
):
    vmem = pl.BlockSpec(memory_space=pltpu.VMEM)
    smem = pl.BlockSpec(memory_space=pltpu.SMEM)
    hbm = pl.BlockSpec(memory_space=pltpu.HBM)
    V = pltpu.VMEM
    scratch = [
        V((2 * C, N), BF16), V((2 * C * H, 128), F32),
        V((9, 4 * CC, 2 * BS), BF16), V((9, 4 * CC, 2 * BS), BF16), V((2 * BS, 2 * N), BF16),
        V((1, 2 * N), jnp.int32), V((1, 2 * N), F32),
        V((CC, 2 * N), F32), V((CC, NP), F32), V((C, N), F32), V((C, N), F32), V((C, N), F32),
        V((C, N), BF16), V((C, N), BF16), V((C, N), BF16), V((C, N), BF16),
        V((3 * C, NP), BF16), V((3 * C, NP), BF16), V((3 * C, NP), BF16), V((3 * C, NP), BF16), V((C, NP), BF16),
        V((3, C, 3 * C), BF16), V((3, C, C), BF16), V((3, C, 3 * C), BF16), V((C, 9 * C), BF16),
        V((3, C, 3 * C), BF16), V((C, 9 * C), BF16), V((3, C, 3 * C), BF16),
        V((7, 2, C, W), BF16), V((7, C, C), BF16), V((7, 32, C), BF16), V((2, 48, W), BF16), V((2, 48, W), BF16),
        V((C, C), BF16), V((16, C), BF16), V((C, C), BF16), V((2 * C, C), BF16), V((16, C), BF16),
        V((2, 64, C), BF16), V((6, 16, C), BF16), V((2, C, C), BF16), V((6, 16, C), BF16),
        V((C, 9 * C), BF16), V((C, 9 * C), BF16),
        V((4, NLAT * NLON, C), F32), V((16 * ROWS_IN, C), F32),
        V((16 * ROWS_IN, C), BF16), V((16 * ROWS_OM, C), BF16), V((8 * ROWS_IN, C), BF16), V((8 * ROWS_OM, C), BF16),
        V((8 * ROWS_IN, C), BF16), V((8 * ROWS_OM, C), BF16), V((8, ROWS_IN, C), BF16), V((8, ROWS_OM, C), BF16),
        V((8, ROWS_IN, C), BF16), V((8, ROWS_OM, C), BF16), V((2, 8, ROWS_IN, C), BF16), V((2, 8, ROWS_OM, C), BF16),
        pltpu.SemaphoreType.DMA((9,)), pltpu.SemaphoreType.DMA((9,)),
        pltpu.SemaphoreType.DMA((7, 8)), pltpu.SemaphoreType.DMA((7, 8)),
        pltpu.SemaphoreType.DMA((4, 2)), pltpu.SemaphoreType.DMA((2, 10)),
    ]
    res = pl.pallas_call(
        kernel,
        out_shape=jax.ShapeDtypeStruct((ROWS, C), BF16),
        in_specs=[vmem, vmem, vmem, smem] + [vmem] * 9,
        out_specs=vmem,
        scratch_shapes=scratch,
        compiler_params=pltpu.CompilerParams(
            collective_id=0, has_side_effects=True, vmem_limit_bytes=56 * 1024 * 1024
        ),
    )(
        features, cotangent, coarse_blocks, send_table, interp_src, interp_wt, jnp.swapaxes(weight_in, 1, 2), weight_mid, weight_out,
        gain_in.reshape(1, C), bias_in.reshape(1, C), gain_mid.reshape(1, C), bias_mid.reshape(1, C),
    )
    field, grad_features, grad_in, grad_mid, grad_out = pl.pallas_call(
        results,
        out_shape=(
            jax.ShapeDtypeStruct((C, H, W), BF16), jax.ShapeDtypeStruct((C, H, W), BF16),
            jax.ShapeDtypeStruct((9, C + CC, C), F32),
            jax.ShapeDtypeStruct((9, C, C), F32), jax.ShapeDtypeStruct((9, C, C), F32),
        ),
        in_specs=[hbm],
        out_specs=(vmem,) * 5,
        scratch_shapes=[V((ROWS, C), BF16), V((C * H, 128), F32), pltpu.SemaphoreType.DMA],
        compiler_params=pltpu.CompilerParams(vmem_limit_bytes=60 * 1024 * 1024),
    )(res)
    return field, grad_features, jnp.swapaxes(grad_in, 1, 2), grad_mid, grad_out


def solution(mesh):
    tile = P(None, "lat", "lon")
    in_specs = (
        tile, P("lon", "lat", None, None), P("lon", None, None, None), tile, tile,
        P(), P(), P(), P(), P(), P(), P(), tile,
    )
    out_specs = (tile, tile, P(), P(), P())
    return jax.shard_map(local, mesh=mesh, in_specs=in_specs, out_specs=out_specs, check_vma=False)
```

```python
import jax
import jax.numpy as jnp
from jax import lax
from jax.experimental import pallas as pl
from jax.experimental.pallas import tpu as pltpu
from jax.sharding import PartitionSpec as P

C = 128
CC = 40
G = 32
H = 8
W = 256
N = H * W
NP = N + 2 * W
BS = 256
SLOT = 8
NLON = 16
NLAT = 8
CELLS = 64 * 4096
MEMBERS = (C // G) * CELLS
FACTOR = CELLS ** -0.5
EPS = 1e-05
ROWS_IN = 96
ROWS_OM = 144
AT_OM = 0
AT_IN = AT_OM + 16 * ROWS_OM
ROWS = AT_IN + 16 * ROWS_IN
F32 = jnp.float32
BF16 = jnp.bfloat16
MESH = pl.DeviceIdType.MESH
FEAT, COT, COND, POOL, MERG, GMID, GIN = range(7)
HOPS = (0, 1, 2, 1)
OTHERS = sorted(
    [(a, b, c, d) for a in range(4) for b in range(4) for c in range(4) for d in range(2) if (a, b, c, d) != (0, 0, 0, 0)],
    key=lambda o: -(HOPS[o[0]] + HOPS[o[1]] + HOPS[o[2]]),
)


def dot(a, b):
    return lax.dot_general(a, b, (((1,), (0,)), ((), ())), preferred_element_type=F32)


def dot_nt(a, b):
    return lax.dot_general(a, b, (((1,), (1,)), ((), ())), preferred_element_type=F32)


def sigmoid(v):
    return 1.0 / (1.0 + jnp.exp(-v))


def kernel(
    feat, cot, blocks, table, src, wt, w_in, w_mid, w_out, gain_in, bias_in, gain_mid, bias_mid,
    fields, res,
    fc, relay, pool_s, pool_r, onehot, fid, fwt, acc, condf, hidden, gmerged, slope, act, merged, gin, up,
    x3f, x3c, x3m, x3g, x3cond, wf, wc, wo, wm, wt_out, wt_mid, wt_in,
    hr, hc, edge, crow, chr_, pooled, pooled_e, gmid, slope_r, slope_e, row_p, pack_p, row_g, pack_g, im_p, im_g,
    gsmall, a1, gw_in, s_in, s_om, core_in, core_om, half_in, half_om, r1_in, r1_om, r2_in, r2_om, full_in, full_om,
    sem_ps, sem_pr, sem_hs, sem_hr, sem_a, sem_b,
):
    lon = lax.axis_index("lon")
    lat = lax.axis_index("lat")

    def at(dlat, dlon):
        return {"lon": lax.rem(lon + dlon + NLON, NLON), "lat": lat + dlat}

    def has_lat(d):
        if d == 0:
            return None
        return jnp.logical_and(lat + d >= 0, lat + d < NLAT)

    def guarded(cond, fn):
        if cond is None:
            fn()
        else:
            pl.when(cond)(fn)

    finish = []

    def send(cond, source, dest, s_sem, r_sem, device):
        copy = pltpu.make_async_remote_copy(
            src_ref=source, dst_ref=dest, send_sem=s_sem, recv_sem=r_sem,
            device_id=device, device_id_type=MESH,
        )
        guarded(cond, copy.start)
        finish.append((cond, copy.wait_send))

    def arrive(ref, sem):
        pltpu.make_async_copy(ref, ref, sem).wait()

    barrier = pltpu.get_barrier_semaphore()

    core = lax.rem(lon, 2)
    chip = lon // 2
    x = lon // 4
    z = lat // 2
    y = lax.rem(chip, 2) * 2 + lax.rem(lat, 2)
    lon_of = {}
    lat_of = {}
    for oy in range(4):
        y2 = lax.rem(y + oy, 4)
        for oc in range(2):
            for ox in range(4):
                lon_of[ox, oy, oc] = (lax.rem(x + ox, 4) * 2 + y2 // 2) * 2 + (core if oc == 0 else 1 - core)
        for oz in range(4):
            lat_of[oz, oy] = lax.rem(z + oz, 4) * 2 + lax.rem(y2, 2)

    def everyone(act_on):
        for ox, oy, oz, oc in OTHERS:
            act_on({"lon": lon_of[ox, oy, oc], "lat": lat_of[oz, oy]})

    everyone(lambda peer: pl.semaphore_signal(barrier, inc=1, device_id=peer, device_id_type=MESH))

    def relaid(ref, base):
        cells = ref[...].astype(F32).reshape(C * H, W)
        for side in range(2):
            relay[side * C * H:(side + 1) * C * H] = cells[:, side * 128:(side + 1) * 128]
            for r in range(H):
                where = slice(r * W + side * 128, r * W + (side + 1) * 128)
                fc[base:base + C, where] = relay[pl.ds(side * C * H + r, C, stride=H), :].astype(BF16)

    relaid(feat, 0)
    relaid(cot, C)

    gaps = [0, 2, -2, 4, -4, 1, -1, 3, -3]

    def pack(k, dest):
        for s2 in range(0, 4, 2):
            for half in range(2):
                one = jnp.maximum(table[0, lat, lat + gaps[k], 2 * s2 + half], 0)
                two = jnp.maximum(table[0, lat, lat + gaps[k], 2 * s2 + 2 + half], 0)
                both = jnp.concatenate([blocks[0, one].astype(F32), blocks[0, two].astype(F32)], axis=0)
                dest[s2 * CC:(s2 + 2) * CC, half * BS:(half + 1) * BS] = both.astype(BF16)

    pack(0, pool_r.at[0])
    for k in range(1, 9):
        guarded(has_lat(gaps[k]), lambda k=k: pack(k, pool_s.at[k]))

    def edge_columns(ref, offset, chans, to):
        lanes = lax.broadcasted_iota(jnp.int32, (chans, 128), 1)
        tile = jnp.zeros((chans, 128), F32)
        for r in range(H):
            base = offset + r * W
            first = ref[:, base:base + 128].astype(F32)
            last = ref[:, base + 128:base + 256].astype(F32)
            tile = jnp.where(lanes == r + 1, first[:, 0:1], tile)
            tile = jnp.where(lanes == r + 17, last[:, 127:128], tile)
        if chans < C:
            tile = jnp.concatenate([tile, jnp.zeros((C - chans, 128), F32)], axis=0)
        to[...] = tile.T[0:32].astype(BF16)

    edge_columns(fc.at[0:C], 0, C, edge.at[FEAT])

    def make_onehot(j, _):
        m = j // H
        r = lax.rem(j, H)
        cells = src[m, pl.ds(r, 1), :]
        low = lax.rem(cells, 2 * BS)
        rows = lax.broadcasted_iota(jnp.int32, (2 * BS, W), 0)
        where = pl.ds(pl.multiple_of(j * W, W), W)
        onehot[:, where] = jnp.where(rows == low, 1.0, 0.0).astype(BF16)
        fid[:, where] = cells // (2 * BS)
        fwt[:, where] = wt[m, pl.ds(r, 1), :]
        return 0

    lax.fori_loop(0, 2 * H, make_onehot, 0)

    for r in range(H):
        small = lax.broadcasted_iota(jnp.int32, (C, W), 0)
        cell = lax.broadcasted_iota(jnp.int32, (C, W), 1)
        up[:, r * W:(r + 1) * W] = jnp.where(small == (r // 4) * 64 + cell // 4, 1.0, 0.0).astype(BF16)

    def turn(t):
        return t.astype(F32).T.astype(BF16)

    for a in range(3):
        rows = []
        for b in range(3):
            t = 3 * a + b
            wf[a, :, b * C:(b + 1) * C] = turn(w_in[t, 0:C, :])
            wo[a, :, b * C:(b + 1) * C] = w_out[t]
            wm[:, t * C:(t + 1) * C] = w_mid[t]
            rows.append(w_in[t, C:C + CC, :].astype(F32))
        wc[a] = jnp.concatenate(rows + [jnp.zeros((8, C), F32)], axis=0).T.astype(BF16)

    def turn_out():
        for t in range(9):
            wt_out[t // 3, :, (t % 3) * C:(t % 3 + 1) * C] = turn(w_out[8 - t])

    def turn_rest():
        for t in range(9):
            wt_mid[:, t * C:(t + 1) * C] = turn(w_mid[8 - t])
            wt_in[t // 3, :, (t % 3) * C:(t % 3 + 1) * C] = w_in[8 - t, 0:C, :]

    turn_out()

    pl.semaphore_wait(barrier, NLAT * NLON - 1)

    def send_fine(f, up_row, down_row, rows_at):
        send(has_lat(-1), up_row, rows_at.at[1], sem_hs.at[f, 0], sem_hr.at[f, 1], at(-1, 0))
        send(has_lat(1), down_row, rows_at.at[0], sem_hs.at[f, 1], sem_hr.at[f, 0], at(1, 0))
        for d in (0, -1, 1):
            left, right = edge.at[f, pl.ds(0, 16)], edge.at[f, pl.ds(16, 16)]
            send(has_lat(d), right, hc.at[f, pl.ds(16 - 16 * d, 16)], sem_hs.at[f, 3 + d], sem_hr.at[f, 3 - d], at(d, 1))
            send(has_lat(d), left, hc.at[f, pl.ds(64 - 16 * d, 16)], sem_hs.at[f, 6 + d], sem_hr.at[f, 6 - d], at(d, -1))

    def send_field(f, ref):
        send_fine(f, ref.at[:, 0:W], ref.at[:, N - W:N], hr.at[f])

    def expect(cond, ref, sem):
        if cond is None:
            arrive(ref, sem)
            return

        @pl.when(cond)
        def _():
            arrive(ref, sem)

        @pl.when(jnp.logical_not(cond))
        def _():
            ref[...] = jnp.zeros(ref.shape, ref.dtype)

    def wait_fine(f, rows_at):
        expect(has_lat(-1), rows_at.at[0], sem_hr.at[f, 0])
        expect(has_lat(1), rows_at.at[1], sem_hr.at[f, 1])
        for d in (0, -1, 1):
            expect(has_lat(d), hc.at[f, pl.ds(16 + 16 * d, 16)], sem_hr.at[f, 3 + d])
            expect(has_lat(d), hc.at[f, pl.ds(64 + 16 * d, 16)], sem_hr.at[f, 6 + d])
        cols = hc[f, 0:96, :].astype(F32)
        return jnp.concatenate([cols, jnp.zeros((32, C), F32)], axis=0).T

    def pool_copy(k):
        back = gaps.index(-gaps[k])
        return pltpu.make_async_remote_copy(
            src_ref=pool_s.at[k], dst_ref=pool_r.at[back], send_sem=sem_ps.at[k], recv_sem=sem_pr.at[back],
            device_id=at(gaps[k], 0), device_id_type=MESH,
        )

    for k in (5, 6, 7, 8, 1, 2, 3, 4):
        copy = pool_copy(k)
        guarded(has_lat(gaps[k]), copy.start)
        finish.append((has_lat(gaps[k]), copy.wait_send))
    send_field(FEAT, fc.at[0:C])

    def left_right(r, cols):
        if r == 0:
            return cols[:, 8:9], cols[:, 56:57]
        if r == H + 1:
            return cols[:, 33:34], cols[:, 81:82]
        return cols[:, 16 + r:17 + r], cols[:, 64 + r:65 + r]

    def shifted(v, r, cols):
        chans = v.shape[0]
        at_lane = lax.broadcasted_iota(jnp.int32, (chans, W), 1)
        first, last = left_right(r, cols)
        before = jnp.where(at_lane == 0, first, pltpu.roll(v, 1, 1))
        after = jnp.where(at_lane == W - 1, last, pltpu.roll(v, W - 1, 1))
        return before, after

    def build(x3, ref, rows_at, cols):
        for r in range(H + 2):
            if r == 0:
                v = rows_at[0]
            elif r == H + 1:
                v = rows_at[1]
            else:
                v = ref[:, (r - 1) * W:r * W]
            before, after = shifted(v.astype(F32), r, cols)
            x3[0:C, r * W:(r + 1) * W] = before.astype(BF16)
            x3[C:2 * C, r * W:(r + 1) * W] = v
            x3[2 * C:3 * C, r * W:(r + 1) * W] = after.astype(BF16)

    STEP = 512

    def conv(weights, x3, use):
        def body(j, _):
            total = None
            for a in range(3):
                start = pl.multiple_of(j * STEP + a * W, W)
                part = dot(weights[a], x3[:, pl.ds(start, STEP)])
                total = part if total is None else total + part
            use(pl.ds(pl.multiple_of(j * STEP, STEP), STEP), total)
            return 0

        lax.fori_loop(0, N // STEP, body, 0)

    def put(ref):
        def use(where, v):
            ref[:, where] = v

        return use

    build(x3f, fc.at[0:C], hr.at[FEAT], wait_fine(FEAT, hr.at[FEAT]))
    conv(wf, x3f, put(hidden))
    def halves(v):
        high = v.astype(BF16)
        return high, (v - high.astype(F32)).astype(BF16)

    acc[...] = jnp.zeros(acc.shape, F32)

    def interp(k, _):
        size = lax.rem(2 * ((k + 1) // 2), 5)
        gap = jnp.where(lax.rem(k, 2) == 1, size, -size)
        owner = lat + gap

        @pl.when(jnp.logical_and(owner >= 0, owner < NLAT))
        def _():
            @pl.when(k > 0)
            def _():
                arrive(pool_r.at[k], sem_pr.at[k])

            products = dot(pool_r[k], onehot[...])
            total = acc[...]
            for s2 in range(4):
                mask = jnp.where(fid[...] == owner * 4 + s2, fwt[...], 0.0)
                total = total + products[s2 * CC:(s2 + 1) * CC] * mask
            acc[...] = total

        return 0

    lax.fori_loop(0, 9, interp, 0)

    blended = acc[:, 0:N] + acc[:, N:2 * N]
    condf[:, W:W + N] = blended.astype(BF16).astype(F32)
    edge_columns(condf, W, CC, edge.at[COND])
    for i, start in enumerate((W, N)):
        row = jnp.concatenate([condf[:, start:start + W], jnp.zeros((8, W), F32)], axis=0)
        crow[i] = row.astype(BF16)
    send_fine(COND, crow.at[0], crow.at[1], chr_)
    cond_cols = wait_fine(COND, chr_)[0:CC]
    for r in range(H + 2):
        if r == 0:
            v = chr_[0].astype(F32)[0:CC]
        elif r == H + 1:
            v = chr_[1].astype(F32)[0:CC]
        else:
            v = condf[:, r * W:(r + 1) * W]
        before, after = shifted(v, r, cond_cols)
        stacked = jnp.concatenate([before, v, after, jnp.zeros((8, W), F32)], axis=0)
        x3cond[:, r * W:(r + 1) * W] = stacked.astype(BF16)

    def add_hidden(where, v):
        hidden[:, where] = hidden[:, where] + v

    conv(wc, x3cond, add_hidden)

    chan = lax.broadcasted_iota(jnp.int32, (C, C), 0)
    other = lax.broadcasted_iota(jnp.int32, (C, C), 1)
    eye = chan == other
    to_first = jnp.where(other == chan // (C // G), 1.0, 0.0)
    to_second = jnp.where(other == G + chan // (C // G), 1.0, 0.0)
    me = lat * NLON + lon

    def to_row(col):
        return jnp.sum(jnp.where(eye, col, 0.0), axis=0, keepdims=True)

    def to_col(row):
        return jnp.sum(jnp.where(eye, row, 0.0), axis=1, keepdims=True)

    def all_sum(k, first, second, beside=None):
        one = jnp.sum(first, axis=1, keepdims=True)
        two = jnp.sum(second, axis=1, keepdims=True)
        mine = a1.at[k, pl.ds(me, 1)]
        a1[k, pl.ds(me, 1), :] = jnp.sum(one * to_first + two * to_second, axis=0, keepdims=True)

        def share(peer):
            pltpu.make_async_remote_copy(
                src_ref=mine, dst_ref=mine, send_sem=sem_a.at[k, 0], recv_sem=sem_a.at[k, 1],
                device_id=peer, device_id_type=MESH,
            ).start()

        everyone(share)
        if beside is not None:
            beside()
        rest = a1.at[k, pl.ds(0, NLAT * NLON - 1)]
        arrive(rest, sem_a.at[k, 1])
        finish.append((None, lambda: arrive(rest, sem_a.at[k, 0])))
        total = jnp.sum(a1[k], axis=0, keepdims=True)
        return (
            jnp.sum(total * to_first, axis=1, keepdims=True),
            jnp.sum(total * to_second, axis=1, keepdims=True),
        )

    def norm_terms(sums, squares, members):
        average = sums / members
        variance = squares / members - average * average
        return average, lax.rsqrt(variance + EPS)

    s = jnp.zeros((C, 128), F32)
    q = jnp.zeros((C, 128), F32)
    for j in range(N // 128):
        v = hidden[:, j * 128:(j + 1) * 128]
        s = s + v
        q = q + v * v
    def beside_first():
        edge_columns(fc.at[C:2 * C], 0, C, edge.at[COT])
        send_field(COT, fc.at[C:2 * C])
        turn_rest()

    sums, squares = all_sum(0, s, q, beside_first)
    avg_in, inv_in = norm_terms(sums, squares, MEMBERS)
    g1 = to_col(gain_in[...])
    b1 = to_col(bias_in[...])
    g2 = to_col(gain_mid[...])
    b2 = to_col(bias_mid[...])

    def activate(j, _):
        where = pl.ds(pl.multiple_of(j * W, W), W)
        affine = g1 * ((hidden[:, where] - avg_in) * inv_in) + b1
        act[:, where] = (affine * sigmoid(affine)).astype(BF16)
        return 0

    lax.fori_loop(0, H, activate, 0)

    def send_coarse(f, rows, near, mine, packs):
        half = rows.shape[0] // 2
        send(has_lat(-1), rows.at[pl.ds(0, half)], near.at[1], sem_hs.at[f, 0], sem_hr.at[f, 1], at(-1, 0))
        send(has_lat(1), rows.at[pl.ds(half, half)], near.at[0], sem_hs.at[f, 1], sem_hr.at[f, 0], at(1, 0))
        for d in (0, -1, 1):
            send(has_lat(d), mine, packs.at[1 - d], sem_hs.at[f, 3 + d], sem_hr.at[f, 3 - d], at(d, 1))
            send(has_lat(d), mine, packs.at[4 - d], sem_hs.at[f, 6 + d], sem_hr.at[f, 6 - d], at(d, -1))

    def wait_coarse(f, near, packs):
        expect(has_lat(-1), near.at[0], sem_hr.at[f, 0])
        expect(has_lat(1), near.at[1], sem_hr.at[f, 1])
        for d in (0, -1, 1):
            expect(has_lat(d), packs.at[1 + d], sem_hr.at[f, 3 + d])
            expect(has_lat(d), packs.at[4 + d], sem_hr.at[f, 6 + d])

    sub16 = lax.broadcasted_iota(jnp.int32, (16, C), 0)

    def corner_rows(v, first, base):
        for i, n in enumerate((0, 64, 63, 127)):
            base = jnp.where(sub16 == first + i, v[n:n + 1], base)
        return base

    def around(own, near, packs, part, first):
        size = 64
        above = near[0].astype(F32)[part * size:(part + 1) * size]
        below = near[1].astype(F32)[part * size:(part + 1) * size]
        full = jnp.concatenate([above, own, below], axis=0)
        ends = [packs[i].astype(F32) for i in range(6)]

        def row(i, n):
            return ends[i][first + n:first + n + 1]

        lefts = [row(0, 3), row(1, 2), row(1, 3), row(2, 2)]
        rights = [row(3, 1), row(4, 0), row(4, 1), row(5, 0)]
        return full, lefts, rights

    cells = lax.broadcasted_iota(jnp.int32, (2 * C, C), 0)

    def build_coarse(im, full, lefts, rights):
        before = pltpu.roll(full, 1, 0)
        after = pltpu.roll(full, 2 * C - 1, 0)
        for k in range(4):
            before = jnp.where(cells == 64 * k, lefts[k], before)
            after = jnp.where(cells == 64 * k + 63, rights[k], after)
        for b, v in enumerate((before, full, after)):
            v = v.astype(BF16)
            for a in range(3):
                im[:, (3 * a + b) * C:(3 * a + b + 1) * C] = v[a * 64:a * 64 + C]

    own = (dot_nt(up[...], act[...]) * (1.0 / 16.0)).astype(BF16)
    pooled[...] = own
    own = own.astype(F32)
    pooled_e[...] = corner_rows(own, 0, jnp.zeros((16, C), F32)).astype(BF16)
    send_coarse(POOL, pooled, row_p, pooled_e, pack_p)
    wait_coarse(POOL, row_p, pack_p)
    build_coarse(im_p, *around(own, row_p, pack_p, 0, 0))
    hidden_mid = dot_nt(wm[...], im_p[...])

    def beside_second():
        build(x3c, fc.at[C:2 * C], hr.at[COT], wait_fine(COT, hr.at[COT]))
        conv(wt_out, x3c, put(gmerged))
        high, low = halves(gmerged[...])
        gsmall[...] = dot_nt(high, up[...]) + dot_nt(low, up[...])

    sums, squares = all_sum(1, hidden_mid, hidden_mid * hidden_mid, beside_second)
    avg_mid, inv_mid = norm_terms(sums, squares, MEMBERS // 16)
    normed_mid = (hidden_mid - avg_mid) * inv_mid
    affine_mid = g2 * normed_mid + b2
    sig = sigmoid(affine_mid)
    act_mid = (affine_mid * sig).astype(BF16)
    slope_mid = gsmall[...] * sig * (1.0 + affine_mid * (1.0 - sig)) * g2
    slope_t = slope_mid.T
    normed_t = normed_mid.T

    def send_slopes():
        for i, n in enumerate((0, 64)):
            slope_r[i * C:i * C + 64] = slope_t[n:n + 64].astype(BF16)
            slope_r[i * C + 64:(i + 1) * C] = normed_t[n:n + 64].astype(BF16)
        ends = corner_rows(slope_t, 0, jnp.zeros((16, C), F32))
        slope_e[...] = corner_rows(normed_t, 4, ends).astype(BF16)
        send_coarse(GMID, slope_r, row_g, slope_e, pack_g)
        for r in range(H):
            where = slice(r * W, (r + 1) * W)
            merged[:, where] = (act[:, where].astype(F32) + dot(act_mid, up[:, where])).astype(BF16)
        edge_columns(merged, 0, C, edge.at[MERG])
        send_field(MERG, merged)

    sum_e, sum_en = all_sum(2, slope_mid, slope_mid * normed_mid, send_slopes)
    mean_e = sum_e / (MEMBERS // 16)
    mean_en = sum_en / (MEMBERS // 16)
    gmid[...] = ((slope_mid - mean_e - normed_mid * mean_en) * inv_mid).astype(BF16)
    wait_coarse(GMID, row_g, pack_g)
    row_e, row_en, row_inv = to_row(mean_e), to_row(mean_en), to_row(inv_mid)
    inside = [jnp.where(lat > 0, 1.0, 0.0), 1.0, 1.0, jnp.where(lat < NLAT - 1, 1.0, 0.0)]

    def settled(e, normed):
        return (e - row_e - normed * row_en) * row_inv

    e_all, e_left, e_right = around(slope_t, row_g, pack_g, 0, 0)
    n_all, n_left, n_right = around(normed_t, row_g, pack_g, 1, 4)
    valid = jnp.where(cells < 64, inside[0], jnp.where(cells < 192, 1.0, inside[3]))
    build_coarse(
        im_g,
        settled(e_all, n_all) * valid,
        [settled(e_left[k], n_left[k]) * inside[k] for k in range(4)],
        [settled(e_right[k], n_right[k]) * inside[k] for k in range(4)],
    )
    gpooled = dot_nt(wt_mid[...], im_g[...]) * (1.0 / 16.0)
    high, low = halves(gpooled)

    def slopes(j, carry):
        s, q = carry
        where = pl.ds(pl.multiple_of(j * W, W), W)
        gact = gmerged[:, where] + dot(high, up[:, where]) + dot(low, up[:, where])
        normed = (hidden[:, where] - avg_in) * inv_in
        affine = g1 * normed + b1
        sig = sigmoid(affine)
        e = gact * sig * (1.0 + affine * (1.0 - sig)) * g1
        slope[:, where] = e
        en = e * normed
        return s + e[:, 0:128] + e[:, 128:256], q + en[:, 0:128] + en[:, 128:256]

    s, q = lax.fori_loop(0, H, slopes, (jnp.zeros((C, 128), F32), jnp.zeros((C, 128), F32)))

    jobs = {
        0: (ROWS_OM, s_om, core_om, half_om, r1_om, r2_om, full_om),
        1: (ROWS_IN, s_in, core_in, half_in, r1_in, r2_in, full_in),
    }
    partner = {"lon": lon + 1 - 2 * core, "lat": lat}

    def pieces(ref, n):
        return ref.at[pl.ds(0, n)]

    def hand(k, step, source, dest, peer):
        pltpu.make_async_remote_copy(
            src_ref=source, dst_ref=dest, send_sem=sem_b.at[k, 2 * step], recv_sem=sem_b.at[k, 2 * step + 1],
            device_id=peer, device_id_type=MESH,
        ).start()

    def along_lon(d):
        return lax.rem(chip + d, NLON // 2)

    def cores(k):
        rows, s_ref, got = jobs[k][:3]
        part = pl.ds(pl.multiple_of((1 - core) * 8 * rows, 16), 8 * rows)
        hand(k, 0, s_ref.at[part], got, partner)
        finish.append((None, lambda: arrive(got, sem_b.at[k, 0])))

    def scatter(k):
        rows, s_ref, got, half, r1 = jobs[k][:5]
        arrive(got, sem_b.at[k, 1])
        part = pl.ds(pl.multiple_of(core * 8 * rows, 16), 8 * rows)
        half[...] = (s_ref[part, :].astype(F32) + got[...].astype(F32)).astype(BF16)
        for d in range(1, 8):
            to = along_lon(d)
            hand(k, 1, half.at[pl.ds(pl.multiple_of(to * rows, 16), rows)], r1.at[chip], {"lon": to * 2 + core, "lat": lat})
        r1[chip] = half[pl.ds(pl.multiple_of(chip * rows, 16), rows), :]
        finish.append((None, lambda: arrive(pieces(r1, 7), sem_b.at[k, 2])))

    def added(ref):
        total = ref[0].astype(F32)
        for i in range(1, 8):
            total = total + ref[i].astype(F32)
        return total.astype(BF16)

    def middle(k):
        r1, r2 = jobs[k][4:6]
        arrive(pieces(r1, 7), sem_b.at[k, 3])
        r2[lat] = added(r1)
        for d in range(1, NLAT):
            hand(k, 2, r2.at[lat], r2.at[lat], {"lon": lon, "lat": lax.rem(lat + d, NLAT)})
        finish.append((None, lambda: arrive(pieces(r2, 7), sem_b.at[k, 4])))

    def gather(k):
        r2, full = jobs[k][5:7]
        arrive(pieces(r2, 7), sem_b.at[k, 5])
        full[core, chip] = added(r2)
        for d in range(1, 8):
            hand(k, 3, full.at[core, chip], full.at[core, chip], {"lon": along_lon(d) * 2 + core, "lat": lat})
        finish.append((None, lambda: arrive(pieces(full.at[core], 7), sem_b.at[k, 6])))

    def exchange(k):
        full = jobs[k][6]
        arrive(pieces(full.at[core], 7), sem_b.at[k, 7])
        hand(k, 4, full.at[core], full.at[core], partner)
        finish.append((None, lambda: arrive(full.at[core], sem_b.at[k, 8])))

    def complete(k, base):
        rows, full = jobs[k][0], jobs[k][6]
        arrive(full.at[1 - core], sem_b.at[k, 9])
        res[base:base + 16 * rows] = full[...].reshape(16 * rows, C)

    def beside_slopes():
        build(x3m, merged, hr.at[MERG], wait_fine(MERG, hr.at[MERG]))
        for a in range(3):
            part = dot_nt(fc[C:2 * C], x3m[:, a * W:a * W + N])
            for b in range(3):
                t = 9 + 3 * a + b
                s_om[t * C:(t + 1) * C] = part[:, b * C:(b + 1) * C].astype(BF16)
        g_mid_w = dot(gmid[...], im_p[...])
        for t in range(9):
            s_om[t * C:(t + 1) * C] = g_mid_w[:, t * C:(t + 1) * C].astype(BF16)
        cores(0)

    sum_e, sum_en = all_sum(3, s, q, beside_slopes)
    scatter(0)
    mean_e = sum_e / MEMBERS
    mean_en = sum_en / MEMBERS

    def finish_in(j, _):
        where = pl.ds(pl.multiple_of(j * W, W), W)
        normed = (hidden[:, where] - avg_in) * inv_in
        gin[:, where] = ((slope[:, where] - mean_e - normed * mean_en) * inv_in).astype(BF16)
        return 0

    lax.fori_loop(0, H, finish_in, 0)

    taps = C + CC
    for a in range(3):
        part = dot_nt(x3f[:, a * W:a * W + N], gin[...])
        more = dot_nt(x3cond[:, a * W:a * W + N], gin[...])
        for b in range(3):
            t = 3 * a + b
            gw_in[t * taps:t * taps + C] = part[b * C:(b + 1) * C]
            gw_in[t * taps + C:(t + 1) * taps] = more[b * CC:(b + 1) * CC]
    gw_in[9 * taps:] = jnp.zeros((16 * ROWS_IN - 9 * taps, C), F32)
    s_in[...] = gw_in[...].astype(BF16)
    cores(1)
    edge_columns(gin, 0, C, edge.at[GIN])
    send_field(GIN, gin)
    scatter(1)

    def put_relaid(where, v):
        for i in range(STEP // 128):
            first = (i % 2) * C * H + where.start // W + i // 2
            relay[pl.ds(first, C, stride=H), :] = v[:, i * 128:(i + 1) * 128]

    def put_field(base):
        for side in range(2):
            cells = relay[side * C * H:(side + 1) * C * H].reshape(C, H, 128)
            fields[base:base + C, :, side * 128:(side + 1) * 128] = cells.astype(BF16)

    def put_out(where, v):
        put_relaid(where, fc[0:C, where].astype(F32) + v)

    conv(wo, x3m, put_out)
    put_field(0)
    middle(0)
    middle(1)
    build(x3g, gin, hr.at[GIN], wait_fine(GIN, hr.at[GIN]))

    def put_feat(where, v):
        put_relaid(where, fc[C:2 * C, where].astype(F32) + v)

    gather(0)
    conv(wt_in, x3g, put_feat)
    put_field(C)
    gather(1)
    exchange(0)
    complete(0, AT_OM)
    exchange(1)
    complete(1, AT_IN)
    for cond, wait in finish:
        guarded(cond, wait)


def results(fields, res_h, field, features, grad_in, grad_mid, grad_out, res, sem):
    moves = [
        pltpu.make_async_copy(a, b, sem.at[i])
        for i, (a, b) in enumerate(((res_h, res), (fields.at[0:C], field), (fields.at[C:2 * C], features)))
    ]
    for move in moves:
        move.start()
    moves[0].wait()
    for t in range(9):
        rows = slice(AT_IN + t * (C + CC), AT_IN + (t + 1) * (C + CC))
        grad_in[t] = res[rows].astype(F32) * FACTOR
        grad_mid[t] = res[AT_OM + t * C:AT_OM + (t + 1) * C].astype(F32) * FACTOR
        grad_out[t] = res[AT_OM + (9 + t) * C:AT_OM + (10 + t) * C].astype(F32) * FACTOR
    for move in moves[1:]:
        move.wait()


def local(
    features, coarse_blocks, send_table, interp_src, interp_wt, weight_in, weight_mid, weight_out,
    gain_in, bias_in, gain_mid, bias_mid, cotangent,
):
    vmem = pl.BlockSpec(memory_space=pltpu.VMEM)
    smem = pl.BlockSpec(memory_space=pltpu.SMEM)
    hbm = pl.BlockSpec(memory_space=pltpu.HBM)
    V = pltpu.VMEM
    scratch = [
        V((2 * C, N), BF16), V((2 * C * H, 128), F32),
        V((9, 4 * CC, 2 * BS), BF16), V((9, 4 * CC, 2 * BS), BF16), V((2 * BS, 2 * N), BF16),
        V((1, 2 * N), jnp.int32), V((1, 2 * N), F32),
        V((CC, 2 * N), F32), V((CC, NP), F32), V((C, N), F32), V((C, N), F32), V((C, N), F32),
        V((C, N), BF16), V((C, N), BF16), V((C, N), BF16), V((C, N), BF16),
        V((3 * C, NP), BF16), V((3 * C, NP), BF16), V((3 * C, NP), BF16), V((3 * C, NP), BF16), V((C, NP), BF16),
        V((3, C, 3 * C), BF16), V((3, C, C), BF16), V((3, C, 3 * C), BF16), V((C, 9 * C), BF16),
        V((3, C, 3 * C), BF16), V((C, 9 * C), BF16), V((3, C, 3 * C), BF16),
        V((7, 2, C, W), BF16), V((7, C, C), BF16), V((7, 32, C), BF16), V((2, 48, W), BF16), V((2, 48, W), BF16),
        V((C, C), BF16), V((16, C), BF16), V((C, C), BF16), V((2 * C, C), BF16), V((16, C), BF16),
        V((2, 64, C), BF16), V((6, 16, C), BF16), V((2, C, C), BF16), V((6, 16, C), BF16),
        V((C, 9 * C), BF16), V((C, 9 * C), BF16),
        V((C, C), F32), V((4, NLAT * NLON, C), F32), V((16 * ROWS_IN, C), F32),
        V((16 * ROWS_IN, C), BF16), V((16 * ROWS_OM, C), BF16), V((8 * ROWS_IN, C), BF16), V((8 * ROWS_OM, C), BF16),
        V((8 * ROWS_IN, C), BF16), V((8 * ROWS_OM, C), BF16), V((8, ROWS_IN, C), BF16), V((8, ROWS_OM, C), BF16),
        V((8, ROWS_IN, C), BF16), V((8, ROWS_OM, C), BF16), V((2, 8, ROWS_IN, C), BF16), V((2, 8, ROWS_OM, C), BF16),
        pltpu.SemaphoreType.DMA((9,)), pltpu.SemaphoreType.DMA((9,)),
        pltpu.SemaphoreType.DMA((7, 8)), pltpu.SemaphoreType.DMA((7, 8)),
        pltpu.SemaphoreType.DMA((4, 2)), pltpu.SemaphoreType.DMA((2, 10)),
    ]
    fields, res = pl.pallas_call(
        kernel,
        out_shape=(jax.ShapeDtypeStruct((2 * C, H, W), BF16), jax.ShapeDtypeStruct((ROWS, C), BF16)),
        in_specs=[vmem, vmem, vmem, smem] + [vmem] * 9,
        out_specs=(vmem, vmem),
        scratch_shapes=scratch,
        compiler_params=pltpu.CompilerParams(
            collective_id=0, has_side_effects=True, vmem_limit_bytes=56 * 1024 * 1024
        ),
    )(
        features, cotangent, coarse_blocks, send_table, interp_src, interp_wt, jnp.swapaxes(weight_in, 1, 2), weight_mid, weight_out,
        gain_in.reshape(1, C), bias_in.reshape(1, C), gain_mid.reshape(1, C), bias_mid.reshape(1, C),
    )
    field, grad_features, grad_in, grad_mid, grad_out = pl.pallas_call(
        results,
        out_shape=(
            jax.ShapeDtypeStruct((C, H, W), BF16), jax.ShapeDtypeStruct((C, H, W), BF16),
            jax.ShapeDtypeStruct((9, C + CC, C), F32),
            jax.ShapeDtypeStruct((9, C, C), F32), jax.ShapeDtypeStruct((9, C, C), F32),
        ),
        in_specs=[hbm, hbm],
        out_specs=(vmem,) * 5,
        scratch_shapes=[V((ROWS, C), BF16), pltpu.SemaphoreType.DMA((3,))],
        compiler_params=pltpu.CompilerParams(vmem_limit_bytes=60 * 1024 * 1024),
    )(fields, res)
    return field, grad_features, jnp.swapaxes(grad_in, 1, 2), grad_mid, grad_out


def solution(mesh):
    tile = P(None, "lat", "lon")
    in_specs = (
        tile, P("lon", "lat", None, None), P("lon", None, None, None), tile, tile,
        P(), P(), P(), P(), P(), P(), P(), tile,
    )
    out_specs = (tile, tile, P(), P(), P())
    return jax.shard_map(local, mesh=mesh, in_specs=in_specs, out_specs=out_specs, check_vma=False)
```

```python
import jax
import jax.numpy as jnp
from jax import lax
from jax.experimental import pallas as pl
from jax.experimental.pallas import tpu as pltpu
from jax.sharding import PartitionSpec as P

C = 128
CC = 40
G = 32
H = 8
W = 256
N = H * W
NP = N + 2 * W
BS = 256
SLOT = 8
NLON = 16
NLAT = 8
CELLS = 64 * 4096
MEMBERS = (C // G) * CELLS
FACTOR = CELLS ** -0.5
EPS = 1e-05
ROWS_IN = 96
ROWS_OM = 144
AT_OM = 0
AT_IN = AT_OM + 16 * ROWS_OM
ROWS = AT_IN + 16 * ROWS_IN
F32 = jnp.float32
BF16 = jnp.bfloat16
MESH = pl.DeviceIdType.MESH
FEAT, COT, COND, POOL, MERG, GMID, GIN = range(7)
HOPS = (0, 1, 2, 1)
OTHERS = sorted(
    [(a, b, c, d) for a in range(4) for b in range(4) for c in range(4) for d in range(2) if (a, b, c, d) != (0, 0, 0, 0)],
    key=lambda o: -(HOPS[o[0]] + HOPS[o[1]] + HOPS[o[2]]),
)


def dot(a, b):
    return lax.dot_general(a, b, (((1,), (0,)), ((), ())), preferred_element_type=F32)


def dot_nt(a, b):
    return lax.dot_general(a, b, (((1,), (1,)), ((), ())), preferred_element_type=F32)


def sigmoid(v):
    return 1.0 / (1.0 + jnp.exp(-v))


def kernel(
    feat, cot, blocks, table, src, wt, w_in, w_mid, w_out, gain_in, bias_in, gain_mid, bias_mid,
    fields, res,
    fc, relay, pool_s, pool_r, onehot, fid, fwt, acc, condf, hidden, gmerged, slope, act, merged, gin, up,
    x3f, x3c, x3m, x3g, x3cond, wf, wc, wo, wm, wt_out, wt_mid, wt_in,
    hr, hc, edge, crow, chr_, pooled, pooled_e, gmid, slope_r, slope_e, row_p, pack_p, row_g, pack_g, im_p, im_g,
    gsmall, a1, gw_in, s_in, s_om, core_in, core_om, half_in, half_om, r1_in, r1_om, r2_in, r2_om, full_in, full_om,
    sem_ps, sem_pr, sem_hs, sem_hr, sem_a, sem_b,
):
    lon = lax.axis_index("lon")
    lat = lax.axis_index("lat")

    def at(dlat, dlon):
        return {"lon": lax.rem(lon + dlon + NLON, NLON), "lat": lat + dlat}

    def has_lat(d):
        if d == 0:
            return None
        return jnp.logical_and(lat + d >= 0, lat + d < NLAT)

    def guarded(cond, fn):
        if cond is None:
            fn()
        else:
            pl.when(cond)(fn)

    finish = []

    def send(cond, source, dest, s_sem, r_sem, device):
        copy = pltpu.make_async_remote_copy(
            src_ref=source, dst_ref=dest, send_sem=s_sem, recv_sem=r_sem,
            device_id=device, device_id_type=MESH,
        )
        guarded(cond, copy.start)
        finish.append((cond, copy.wait_send))

    def arrive(ref, sem):
        pltpu.make_async_copy(ref, ref, sem).wait()

    barrier = pltpu.get_barrier_semaphore()

    core = lax.rem(lon, 2)
    chip = lon // 2
    x = lon // 4
    z = lat // 2
    y = lax.rem(chip, 2) * 2 + lax.rem(lat, 2)
    lon_of = {}
    lat_of = {}
    for oy in range(4):
        y2 = lax.rem(y + oy, 4)
        for oc in range(2):
            for ox in range(4):
                lon_of[ox, oy, oc] = (lax.rem(x + ox, 4) * 2 + y2 // 2) * 2 + (core if oc == 0 else 1 - core)
        for oz in range(4):
            lat_of[oz, oy] = lax.rem(z + oz, 4) * 2 + lax.rem(y2, 2)

    def everyone(act_on):
        for ox, oy, oz, oc in OTHERS:
            act_on({"lon": lon_of[ox, oy, oc], "lat": lat_of[oz, oy]})

    everyone(lambda peer: pl.semaphore_signal(barrier, inc=1, device_id=peer, device_id_type=MESH))

    def relaid(ref, base):
        cells = ref[...].astype(F32).reshape(C * H, W)
        for side in range(2):
            relay[side * C * H:(side + 1) * C * H] = cells[:, side * 128:(side + 1) * 128]
            for r in range(H):
                where = slice(r * W + side * 128, r * W + (side + 1) * 128)
                fc[base:base + C, where] = relay[pl.ds(side * C * H + r, C, stride=H), :].astype(BF16)

    relaid(feat, 0)
    relaid(cot, C)

    gaps = [0, 2, -2, 4, -4, 1, -1, 3, -3]

    def pack(k, dest):
        for s2 in range(0, 4, 2):
            for half in range(2):
                one = jnp.maximum(table[0, lat, lat + gaps[k], 2 * s2 + half], 0)
                two = jnp.maximum(table[0, lat, lat + gaps[k], 2 * s2 + 2 + half], 0)
                both = jnp.concatenate([blocks[0, one].astype(F32), blocks[0, two].astype(F32)], axis=0)
                dest[s2 * CC:(s2 + 2) * CC, half * BS:(half + 1) * BS] = both.astype(BF16)

    pack(0, pool_r.at[0])
    for k in range(1, 9):
        guarded(has_lat(gaps[k]), lambda k=k: pack(k, pool_s.at[k]))

    def edge_columns(ref, offset, chans, to):
        lanes = lax.broadcasted_iota(jnp.int32, (chans, 128), 1)
        tile = jnp.zeros((chans, 128), F32)
        for r in range(H):
            base = offset + r * W
            first = ref[:, base:base + 128].astype(F32)
            last = ref[:, base + 128:base + 256].astype(F32)
            tile = jnp.where(lanes == r + 1, first[:, 0:1], tile)
            tile = jnp.where(lanes == r + 17, last[:, 127:128], tile)
        if chans < C:
            tile = jnp.concatenate([tile, jnp.zeros((C - chans, 128), F32)], axis=0)
        to[...] = tile.T[0:32].astype(BF16)

    edge_columns(fc.at[0:C], 0, C, edge.at[FEAT])

    def make_onehot(j, _):
        m = j // H
        r = lax.rem(j, H)
        cells = src[m, pl.ds(r, 1), :]
        low = lax.rem(cells, 2 * BS)
        rows = lax.broadcasted_iota(jnp.int32, (2 * BS, W), 0)
        where = pl.ds(pl.multiple_of(j * W, W), W)
        onehot[:, where] = jnp.where(rows == low, 1.0, 0.0).astype(BF16)
        fid[:, where] = cells // (2 * BS)
        fwt[:, where] = wt[m, pl.ds(r, 1), :]
        return 0

    lax.fori_loop(0, 2 * H, make_onehot, 0)

    for r in range(H):
        small = lax.broadcasted_iota(jnp.int32, (C, W), 0)
        cell = lax.broadcasted_iota(jnp.int32, (C, W), 1)
        up[:, r * W:(r + 1) * W] = jnp.where(small == (r // 4) * 64 + cell // 4, 1.0, 0.0).astype(BF16)

    def turn(t):
        return t.astype(F32).T.astype(BF16)

    for a in range(3):
        rows = []
        for b in range(3):
            t = 3 * a + b
            wf[a, :, b * C:(b + 1) * C] = turn(w_in[t, 0:C, :])
            wo[a, :, b * C:(b + 1) * C] = w_out[t]
            wm[:, t * C:(t + 1) * C] = w_mid[t]
            rows.append(w_in[t, C:C + CC, :].astype(F32))
        wc[a] = jnp.concatenate(rows + [jnp.zeros((8, C), F32)], axis=0).T.astype(BF16)

    def turn_out():
        for t in range(9):
            wt_out[t // 3, :, (t % 3) * C:(t % 3 + 1) * C] = turn(w_out[8 - t])

    def turn_rest():
        for t in range(9):
            wt_mid[:, t * C:(t + 1) * C] = turn(w_mid[8 - t])
            wt_in[t // 3, :, (t % 3) * C:(t % 3 + 1) * C] = w_in[8 - t, 0:C, :]

    turn_out()

    pl.semaphore_wait(barrier, NLAT * NLON - 1)

    def send_fine(f, up_row, down_row, rows_at):
        send(has_lat(-1), up_row, rows_at.at[1], sem_hs.at[f, 0], sem_hr.at[f, 1], at(-1, 0))
        send(has_lat(1), down_row, rows_at.at[0], sem_hs.at[f, 1], sem_hr.at[f, 0], at(1, 0))
        for d in (0, -1, 1):
            left, right = edge.at[f, pl.ds(0, 16)], edge.at[f, pl.ds(16, 16)]
            send(has_lat(d), right, hc.at[f, pl.ds(16 - 16 * d, 16)], sem_hs.at[f, 3 + d], sem_hr.at[f, 3 - d], at(d, 1))
            send(has_lat(d), left, hc.at[f, pl.ds(64 - 16 * d, 16)], sem_hs.at[f, 6 + d], sem_hr.at[f, 6 - d], at(d, -1))

    def send_field(f, ref):
        send_fine(f, ref.at[:, 0:W], ref.at[:, N - W:N], hr.at[f])

    def expect(cond, ref, sem):
        if cond is None:
            arrive(ref, sem)
            return

        @pl.when(cond)
        def _():
            arrive(ref, sem)

        @pl.when(jnp.logical_not(cond))
        def _():
            ref[...] = jnp.zeros(ref.shape, ref.dtype)

    def wait_fine(f, rows_at):
        expect(has_lat(-1), rows_at.at[0], sem_hr.at[f, 0])
        expect(has_lat(1), rows_at.at[1], sem_hr.at[f, 1])
        for d in (0, -1, 1):
            expect(has_lat(d), hc.at[f, pl.ds(16 + 16 * d, 16)], sem_hr.at[f, 3 + d])
            expect(has_lat(d), hc.at[f, pl.ds(64 + 16 * d, 16)], sem_hr.at[f, 6 + d])
        cols = hc[f, 0:96, :].astype(F32)
        return jnp.concatenate([cols, jnp.zeros((32, C), F32)], axis=0).T

    def pool_copy(k):
        back = gaps.index(-gaps[k])
        return pltpu.make_async_remote_copy(
            src_ref=pool_s.at[k], dst_ref=pool_r.at[back], send_sem=sem_ps.at[k], recv_sem=sem_pr.at[back],
            device_id=at(gaps[k], 0), device_id_type=MESH,
        )

    for k in (5, 6, 7, 8, 1, 2, 3, 4):
        copy = pool_copy(k)
        guarded(has_lat(gaps[k]), copy.start)
        finish.append((has_lat(gaps[k]), copy.wait_send))
    send_field(FEAT, fc.at[0:C])

    def left_right(r, cols):
        if r == 0:
            return cols[:, 8:9], cols[:, 56:57]
        if r == H + 1:
            return cols[:, 33:34], cols[:, 81:82]
        return cols[:, 16 + r:17 + r], cols[:, 64 + r:65 + r]

    def shifted(v, r, cols):
        chans = v.shape[0]
        at_lane = lax.broadcasted_iota(jnp.int32, (chans, W), 1)
        first, last = left_right(r, cols)
        before = jnp.where(at_lane == 0, first, pltpu.roll(v, 1, 1))
        after = jnp.where(at_lane == W - 1, last, pltpu.roll(v, W - 1, 1))
        return before, after

    def build(x3, ref, rows_at, cols):
        for r in range(H + 2):
            if r == 0:
                v = rows_at[0]
            elif r == H + 1:
                v = rows_at[1]
            else:
                v = ref[:, (r - 1) * W:r * W]
            before, after = shifted(v.astype(F32), r, cols)
            x3[0:C, r * W:(r + 1) * W] = before.astype(BF16)
            x3[C:2 * C, r * W:(r + 1) * W] = v
            x3[2 * C:3 * C, r * W:(r + 1) * W] = after.astype(BF16)

    STEP = 512

    def conv(weights, x3, use):
        def body(j, _):
            total = None
            for a in range(3):
                start = pl.multiple_of(j * STEP + a * W, W)
                part = dot(weights[a], x3[:, pl.ds(start, STEP)])
                total = part if total is None else total + part
            use(pl.ds(pl.multiple_of(j * STEP, STEP), STEP), total)
            return 0

        lax.fori_loop(0, N // STEP, body, 0)

    def put(ref):
        def use(where, v):
            ref[:, where] = v

        return use

    build(x3f, fc.at[0:C], hr.at[FEAT], wait_fine(FEAT, hr.at[FEAT]))
    conv(wf, x3f, put(hidden))
    def halves(v):
        high = v.astype(BF16)
        return high, (v - high.astype(F32)).astype(BF16)

    acc[...] = jnp.zeros(acc.shape, F32)

    def interp(k, _):
        size = lax.rem(2 * ((k + 1) // 2), 5)
        gap = jnp.where(lax.rem(k, 2) == 1, size, -size)
        owner = lat + gap

        @pl.when(jnp.logical_and(owner >= 0, owner < NLAT))
        def _():
            @pl.when(k > 0)
            def _():
                arrive(pool_r.at[k], sem_pr.at[k])

            products = dot(pool_r[k], onehot[...])
            total = acc[...]
            for s2 in range(4):
                mask = jnp.where(fid[...] == owner * 4 + s2, fwt[...], 0.0)
                total = total + products[s2 * CC:(s2 + 1) * CC] * mask
            acc[...] = total

        return 0

    lax.fori_loop(0, 9, interp, 0)

    blended = acc[:, 0:N] + acc[:, N:2 * N]
    condf[:, W:W + N] = blended.astype(BF16).astype(F32)
    edge_columns(condf, W, CC, edge.at[COND])
    for i, start in enumerate((W, N)):
        row = jnp.concatenate([condf[:, start:start + W], jnp.zeros((8, W), F32)], axis=0)
        crow[i] = row.astype(BF16)
    send_fine(COND, crow.at[0], crow.at[1], chr_)
    cond_cols = wait_fine(COND, chr_)[0:CC]
    for r in range(H + 2):
        if r == 0:
            v = chr_[0].astype(F32)[0:CC]
        elif r == H + 1:
            v = chr_[1].astype(F32)[0:CC]
        else:
            v = condf[:, r * W:(r + 1) * W]
        before, after = shifted(v, r, cond_cols)
        stacked = jnp.concatenate([before, v, after, jnp.zeros((8, W), F32)], axis=0)
        x3cond[:, r * W:(r + 1) * W] = stacked.astype(BF16)

    def add_hidden(where, v):
        hidden[:, where] = hidden[:, where] + v

    conv(wc, x3cond, add_hidden)

    chan = lax.broadcasted_iota(jnp.int32, (C, C), 0)
    other = lax.broadcasted_iota(jnp.int32, (C, C), 1)
    eye = chan == other
    to_first = jnp.where(other == chan // (C // G), 1.0, 0.0)
    to_second = jnp.where(other == G + chan // (C // G), 1.0, 0.0)
    me = lat * NLON + lon

    def to_row(col):
        return jnp.sum(jnp.where(eye, col, 0.0), axis=0, keepdims=True)

    def to_col(row):
        return jnp.sum(jnp.where(eye, row, 0.0), axis=1, keepdims=True)

    def all_sum(k, first, second, beside=None):
        one = jnp.sum(first, axis=1, keepdims=True)
        two = jnp.sum(second, axis=1, keepdims=True)
        mine = a1.at[k, pl.ds(me, 1)]
        a1[k, pl.ds(me, 1), :] = jnp.sum(one * to_first + two * to_second, axis=0, keepdims=True)

        def share(peer):
            pltpu.make_async_remote_copy(
                src_ref=mine, dst_ref=mine, send_sem=sem_a.at[k, 0], recv_sem=sem_a.at[k, 1],
                device_id=peer, device_id_type=MESH,
            ).start()

        everyone(share)
        if beside is not None:
            beside()
        rest = a1.at[k, pl.ds(0, NLAT * NLON - 1)]
        arrive(rest, sem_a.at[k, 1])
        finish.append((None, lambda: arrive(rest, sem_a.at[k, 0])))
        total = jnp.sum(a1[k], axis=0, keepdims=True)
        return (
            jnp.sum(total * to_first, axis=1, keepdims=True),
            jnp.sum(total * to_second, axis=1, keepdims=True),
        )

    def norm_terms(sums, squares, members):
        average = sums / members
        variance = squares / members - average * average
        return average, lax.rsqrt(variance + EPS)

    s = jnp.zeros((C, 128), F32)
    q = jnp.zeros((C, 128), F32)
    for j in range(N // 128):
        v = hidden[:, j * 128:(j + 1) * 128]
        s = s + v
        q = q + v * v
    def beside_first():
        edge_columns(fc.at[C:2 * C], 0, C, edge.at[COT])
        send_field(COT, fc.at[C:2 * C])
        turn_rest()

    sums, squares = all_sum(0, s, q, beside_first)
    avg_in, inv_in = norm_terms(sums, squares, MEMBERS)
    g1 = to_col(gain_in[...])
    b1 = to_col(bias_in[...])
    g2 = to_col(gain_mid[...])
    b2 = to_col(bias_mid[...])

    def activate(j, _):
        where = pl.ds(pl.multiple_of(j * W, W), W)
        affine = g1 * ((hidden[:, where] - avg_in) * inv_in) + b1
        act[:, where] = (affine * sigmoid(affine)).astype(BF16)
        return 0

    lax.fori_loop(0, H, activate, 0)

    def send_coarse(f, rows, near, mine, packs):
        half = rows.shape[0] // 2
        send(has_lat(-1), rows.at[pl.ds(0, half)], near.at[1], sem_hs.at[f, 0], sem_hr.at[f, 1], at(-1, 0))
        send(has_lat(1), rows.at[pl.ds(half, half)], near.at[0], sem_hs.at[f, 1], sem_hr.at[f, 0], at(1, 0))
        for d in (0, -1, 1):
            send(has_lat(d), mine, packs.at[1 - d], sem_hs.at[f, 3 + d], sem_hr.at[f, 3 - d], at(d, 1))
            send(has_lat(d), mine, packs.at[4 - d], sem_hs.at[f, 6 + d], sem_hr.at[f, 6 - d], at(d, -1))

    def wait_coarse(f, near, packs):
        expect(has_lat(-1), near.at[0], sem_hr.at[f, 0])
        expect(has_lat(1), near.at[1], sem_hr.at[f, 1])
        for d in (0, -1, 1):
            expect(has_lat(d), packs.at[1 + d], sem_hr.at[f, 3 + d])
            expect(has_lat(d), packs.at[4 + d], sem_hr.at[f, 6 + d])

    sub16 = lax.broadcasted_iota(jnp.int32, (16, C), 0)

    def corner_rows(v, first, base):
        for i, n in enumerate((0, 64, 63, 127)):
            base = jnp.where(sub16 == first + i, v[n:n + 1], base)
        return base

    def around(own, near, packs, part, first):
        size = 64
        above = near[0].astype(F32)[part * size:(part + 1) * size]
        below = near[1].astype(F32)[part * size:(part + 1) * size]
        full = jnp.concatenate([above, own, below], axis=0)
        ends = [packs[i].astype(F32) for i in range(6)]

        def row(i, n):
            return ends[i][first + n:first + n + 1]

        lefts = [row(0, 3), row(1, 2), row(1, 3), row(2, 2)]
        rights = [row(3, 1), row(4, 0), row(4, 1), row(5, 0)]
        return full, lefts, rights

    cells = lax.broadcasted_iota(jnp.int32, (2 * C, C), 0)

    def build_coarse(im, full, lefts, rights):
        before = pltpu.roll(full, 1, 0)
        after = pltpu.roll(full, 2 * C - 1, 0)
        for k in range(4):
            before = jnp.where(cells == 64 * k, lefts[k], before)
            after = jnp.where(cells == 64 * k + 63, rights[k], after)
        for b, v in enumerate((before, full, after)):
            v = v.astype(BF16)
            for a in range(3):
                im[:, (3 * a + b) * C:(3 * a + b + 1) * C] = v[a * 64:a * 64 + C]

    own = (dot_nt(up[...], act[...]) * (1.0 / 16.0)).astype(BF16)
    pooled[...] = own
    own = own.astype(F32)
    pooled_e[...] = corner_rows(own, 0, jnp.zeros((16, C), F32)).astype(BF16)
    send_coarse(POOL, pooled, row_p, pooled_e, pack_p)
    wait_coarse(POOL, row_p, pack_p)
    build_coarse(im_p, *around(own, row_p, pack_p, 0, 0))
    hidden_mid = dot_nt(wm[...], im_p[...])

    def beside_second():
        build(x3c, fc.at[C:2 * C], hr.at[COT], wait_fine(COT, hr.at[COT]))
        conv(wt_out, x3c, put(gmerged))
        high, low = halves(gmerged[...])
        gsmall[...] = dot_nt(high, up[...]) + dot_nt(low, up[...])

    sums, squares = all_sum(1, hidden_mid, hidden_mid * hidden_mid, beside_second)
    avg_mid, inv_mid = norm_terms(sums, squares, MEMBERS // 16)
    normed_mid = (hidden_mid - avg_mid) * inv_mid
    affine_mid = g2 * normed_mid + b2
    sig = sigmoid(affine_mid)
    act_mid = (affine_mid * sig).astype(BF16)
    slope_mid = gsmall[...] * sig * (1.0 + affine_mid * (1.0 - sig)) * g2
    slope_t = slope_mid.T
    normed_t = normed_mid.T

    def send_slopes():
        for i, n in enumerate((0, 64)):
            slope_r[i * C:i * C + 64] = slope_t[n:n + 64].astype(BF16)
            slope_r[i * C + 64:(i + 1) * C] = normed_t[n:n + 64].astype(BF16)
        ends = corner_rows(slope_t, 0, jnp.zeros((16, C), F32))
        slope_e[...] = corner_rows(normed_t, 4, ends).astype(BF16)
        send_coarse(GMID, slope_r, row_g, slope_e, pack_g)
        for r in range(H):
            where = slice(r * W, (r + 1) * W)
            merged[:, where] = (act[:, where].astype(F32) + dot(act_mid, up[:, where])).astype(BF16)
        edge_columns(merged, 0, C, edge.at[MERG])
        send_field(MERG, merged)

    sum_e, sum_en = all_sum(2, slope_mid, slope_mid * normed_mid, send_slopes)
    mean_e = sum_e / (MEMBERS // 16)
    mean_en = sum_en / (MEMBERS // 16)
    gmid[...] = ((slope_mid - mean_e - normed_mid * mean_en) * inv_mid).astype(BF16)
    wait_coarse(GMID, row_g, pack_g)
    row_e, row_en, row_inv = to_row(mean_e), to_row(mean_en), to_row(inv_mid)
    inside = [jnp.where(lat > 0, 1.0, 0.0), 1.0, 1.0, jnp.where(lat < NLAT - 1, 1.0, 0.0)]

    def settled(e, normed):
        return (e - row_e - normed * row_en) * row_inv

    e_all, e_left, e_right = around(slope_t, row_g, pack_g, 0, 0)
    n_all, n_left, n_right = around(normed_t, row_g, pack_g, 1, 4)
    valid = jnp.where(cells < 64, inside[0], jnp.where(cells < 192, 1.0, inside[3]))
    build_coarse(
        im_g,
        settled(e_all, n_all) * valid,
        [settled(e_left[k], n_left[k]) * inside[k] for k in range(4)],
        [settled(e_right[k], n_right[k]) * inside[k] for k in range(4)],
    )
    gpooled = dot_nt(wt_mid[...], im_g[...]) * (1.0 / 16.0)
    high, low = halves(gpooled)

    def slopes(j, carry):
        s, q = carry
        where = pl.ds(pl.multiple_of(j * W, W), W)
        gact = gmerged[:, where] + dot(high, up[:, where]) + dot(low, up[:, where])
        normed = (hidden[:, where] - avg_in) * inv_in
        affine = g1 * normed + b1
        sig = sigmoid(affine)
        e = gact * sig * (1.0 + affine * (1.0 - sig)) * g1
        slope[:, where] = e
        en = e * normed
        return s + e[:, 0:128] + e[:, 128:256], q + en[:, 0:128] + en[:, 128:256]

    s, q = lax.fori_loop(0, H, slopes, (jnp.zeros((C, 128), F32), jnp.zeros((C, 128), F32)))

    jobs = {
        0: (ROWS_OM, s_om, core_om, half_om, r1_om, r2_om, full_om),
        1: (ROWS_IN, s_in, core_in, half_in, r1_in, r2_in, full_in),
    }
    partner = {"lon": lon + 1 - 2 * core, "lat": lat}

    def pieces(ref, n):
        return ref.at[pl.ds(0, n)]

    def hand(k, step, source, dest, peer):
        pltpu.make_async_remote_copy(
            src_ref=source, dst_ref=dest, send_sem=sem_b.at[k, 2 * step], recv_sem=sem_b.at[k, 2 * step + 1],
            device_id=peer, device_id_type=MESH,
        ).start()

    def along_lon(d):
        return lax.rem(chip + d, NLON // 2)

    def cores(k):
        rows, s_ref, got = jobs[k][:3]
        part = pl.ds(pl.multiple_of((1 - core) * 8 * rows, 16), 8 * rows)
        hand(k, 0, s_ref.at[part], got, partner)
        finish.append((None, lambda: arrive(got, sem_b.at[k, 0])))

    def scatter(k):
        rows, s_ref, got, half, r1 = jobs[k][:5]
        arrive(got, sem_b.at[k, 1])
        part = pl.ds(pl.multiple_of(core * 8 * rows, 16), 8 * rows)
        half[...] = (s_ref[part, :].astype(F32) + got[...].astype(F32)).astype(BF16)
        for d in range(1, 8):
            to = along_lon(d)
            hand(k, 1, half.at[pl.ds(pl.multiple_of(to * rows, 16), rows)], r1.at[chip], {"lon": to * 2 + core, "lat": lat})
        r1[chip] = half[pl.ds(pl.multiple_of(chip * rows, 16), rows), :]
        finish.append((None, lambda: arrive(pieces(r1, 7), sem_b.at[k, 2])))

    def added(ref):
        total = ref[0].astype(F32)
        for i in range(1, 8):
            total = total + ref[i].astype(F32)
        return total.astype(BF16)

    def middle(k):
        r1, r2 = jobs[k][4:6]
        arrive(pieces(r1, 7), sem_b.at[k, 3])
        r2[lat] = added(r1)
        for d in range(1, NLAT):
            hand(k, 2, r2.at[lat], r2.at[lat], {"lon": lon, "lat": lax.rem(lat + d, NLAT)})
        finish.append((None, lambda: arrive(pieces(r2, 7), sem_b.at[k, 4])))

    def gather(k):
        r2, full = jobs[k][5:7]
        arrive(pieces(r2, 7), sem_b.at[k, 5])
        full[core, chip] = added(r2)
        for d in range(1, 8):
            hand(k, 3, full.at[core, chip], full.at[core, chip], {"lon": along_lon(d) * 2 + core, "lat": lat})
        finish.append((None, lambda: arrive(pieces(full.at[core], 7), sem_b.at[k, 6])))

    def exchange(k):
        full = jobs[k][6]
        arrive(pieces(full.at[core], 7), sem_b.at[k, 7])
        hand(k, 4, full.at[core], full.at[core], partner)
        finish.append((None, lambda: arrive(full.at[core], sem_b.at[k, 8])))

    def complete(k, base):
        rows, full = jobs[k][0], jobs[k][6]
        arrive(full.at[1 - core], sem_b.at[k, 9])
        res[base:base + 16 * rows] = full[...].reshape(16 * rows, C)

    def beside_slopes():
        build(x3m, merged, hr.at[MERG], wait_fine(MERG, hr.at[MERG]))
        for a in range(3):
            part = dot_nt(fc[C:2 * C], x3m[:, a * W:a * W + N])
            for b in range(3):
                t = 9 + 3 * a + b
                s_om[t * C:(t + 1) * C] = part[:, b * C:(b + 1) * C].astype(BF16)
        g_mid_w = dot(gmid[...], im_p[...])
        for t in range(9):
            s_om[t * C:(t + 1) * C] = g_mid_w[:, t * C:(t + 1) * C].astype(BF16)
        cores(0)

    sum_e, sum_en = all_sum(3, s, q, beside_slopes)
    scatter(0)
    mean_e = sum_e / MEMBERS
    mean_en = sum_en / MEMBERS

    def finish_in(j, _):
        where = pl.ds(pl.multiple_of(j * W, W), W)
        normed = (hidden[:, where] - avg_in) * inv_in
        gin[:, where] = ((slope[:, where] - mean_e - normed * mean_en) * inv_in).astype(BF16)
        return 0

    lax.fori_loop(0, H, finish_in, 0)

    taps = C + CC
    for a in range(3):
        part = dot_nt(x3f[:, a * W:a * W + N], gin[...])
        more = dot_nt(x3cond[:, a * W:a * W + N], gin[...])
        for b in range(3):
            t = 3 * a + b
            gw_in[t * taps:t * taps + C] = part[b * C:(b + 1) * C]
            gw_in[t * taps + C:(t + 1) * taps] = more[b * CC:(b + 1) * CC]
    gw_in[9 * taps:] = jnp.zeros((16 * ROWS_IN - 9 * taps, C), F32)
    s_in[...] = gw_in[...].astype(BF16)
    cores(1)
    edge_columns(gin, 0, C, edge.at[GIN])
    send_field(GIN, gin)
    scatter(1)

    def put_relaid(where, v):
        for i in range(STEP // 128):
            first = (i % 2) * C * H + where.start // W + i // 2
            relay[pl.ds(first, C, stride=H), :] = v[:, i * 128:(i + 1) * 128]

    def put_field(base):
        for side in range(2):
            cells = relay[side * C * H:(side + 1) * C * H].reshape(C, H, 128)
            fields[base:base + C, :, side * 128:(side + 1) * 128] = cells.astype(BF16)

    def put_out(where, v):
        put_relaid(where, fc[0:C, where].astype(F32) + v)

    def put_feat(where, v):
        put_relaid(where, fc[C:2 * C, where].astype(F32) + v)

    middle(0)
    conv(wo, x3m, put_out)
    put_field(0)
    middle(1)
    gather(0)
    build(x3g, gin, hr.at[GIN], wait_fine(GIN, hr.at[GIN]))
    conv(wt_in, x3g, put_feat)
    put_field(C)
    gather(1)
    exchange(0)
    complete(0, AT_OM)
    exchange(1)
    complete(1, AT_IN)
    for cond, wait in finish:
        guarded(cond, wait)


def results(fields, res_h, field, features, grad_in, grad_mid, grad_out, res, sem):
    moves = [
        pltpu.make_async_copy(a, b, sem.at[i])
        for i, (a, b) in enumerate(((res_h, res), (fields.at[0:C], field), (fields.at[C:2 * C], features)))
    ]
    for move in moves:
        move.start()
    moves[0].wait()
    for t in range(9):
        rows = slice(AT_IN + t * (C + CC), AT_IN + (t + 1) * (C + CC))
        grad_in[t] = res[rows].astype(F32) * FACTOR
        grad_mid[t] = res[AT_OM + t * C:AT_OM + (t + 1) * C].astype(F32) * FACTOR
        grad_out[t] = res[AT_OM + (9 + t) * C:AT_OM + (10 + t) * C].astype(F32) * FACTOR
    for move in moves[1:]:
        move.wait()


def local(
    features, coarse_blocks, send_table, interp_src, interp_wt, weight_in, weight_mid, weight_out,
    gain_in, bias_in, gain_mid, bias_mid, cotangent,
):
    vmem = pl.BlockSpec(memory_space=pltpu.VMEM)
    smem = pl.BlockSpec(memory_space=pltpu.SMEM)
    hbm = pl.BlockSpec(memory_space=pltpu.HBM)
    V = pltpu.VMEM
    scratch = [
        V((2 * C, N), BF16), V((2 * C * H, 128), F32),
        V((9, 4 * CC, 2 * BS), BF16), V((9, 4 * CC, 2 * BS), BF16), V((2 * BS, 2 * N), BF16),
        V((1, 2 * N), jnp.int32), V((1, 2 * N), F32),
        V((CC, 2 * N), F32), V((CC, NP), F32), V((C, N), F32), V((C, N), F32), V((C, N), F32),
        V((C, N), BF16), V((C, N), BF16), V((C, N), BF16), V((C, N), BF16),
        V((3 * C, NP), BF16), V((3 * C, NP), BF16), V((3 * C, NP), BF16), V((3 * C, NP), BF16), V((C, NP), BF16),
        V((3, C, 3 * C), BF16), V((3, C, C), BF16), V((3, C, 3 * C), BF16), V((C, 9 * C), BF16),
        V((3, C, 3 * C), BF16), V((C, 9 * C), BF16), V((3, C, 3 * C), BF16),
        V((7, 2, C, W), BF16), V((7, C, C), BF16), V((7, 32, C), BF16), V((2, 48, W), BF16), V((2, 48, W), BF16),
        V((C, C), BF16), V((16, C), BF16), V((C, C), BF16), V((2 * C, C), BF16), V((16, C), BF16),
        V((2, 64, C), BF16), V((6, 16, C), BF16), V((2, C, C), BF16), V((6, 16, C), BF16),
        V((C, 9 * C), BF16), V((C, 9 * C), BF16),
        V((C, C), F32), V((4, NLAT * NLON, C), F32), V((16 * ROWS_IN, C), F32),
        V((16 * ROWS_IN, C), BF16), V((16 * ROWS_OM, C), BF16), V((8 * ROWS_IN, C), BF16), V((8 * ROWS_OM, C), BF16),
        V((8 * ROWS_IN, C), BF16), V((8 * ROWS_OM, C), BF16), V((8, ROWS_IN, C), BF16), V((8, ROWS_OM, C), BF16),
        V((8, ROWS_IN, C), BF16), V((8, ROWS_OM, C), BF16), V((2, 8, ROWS_IN, C), BF16), V((2, 8, ROWS_OM, C), BF16),
        pltpu.SemaphoreType.DMA((9,)), pltpu.SemaphoreType.DMA((9,)),
        pltpu.SemaphoreType.DMA((7, 8)), pltpu.SemaphoreType.DMA((7, 8)),
        pltpu.SemaphoreType.DMA((4, 2)), pltpu.SemaphoreType.DMA((2, 10)),
    ]
    fields, res = pl.pallas_call(
        kernel,
        out_shape=(jax.ShapeDtypeStruct((2 * C, H, W), BF16), jax.ShapeDtypeStruct((ROWS, C), BF16)),
        in_specs=[vmem, vmem, vmem, smem] + [vmem] * 9,
        out_specs=(vmem, vmem),
        scratch_shapes=scratch,
        compiler_params=pltpu.CompilerParams(
            collective_id=0, has_side_effects=True, vmem_limit_bytes=56 * 1024 * 1024
        ),
    )(
        features, cotangent, coarse_blocks, send_table, interp_src, interp_wt, jnp.swapaxes(weight_in, 1, 2), weight_mid, weight_out,
        gain_in.reshape(1, C), bias_in.reshape(1, C), gain_mid.reshape(1, C), bias_mid.reshape(1, C),
    )
    field, grad_features, grad_in, grad_mid, grad_out = pl.pallas_call(
        results,
        out_shape=(
            jax.ShapeDtypeStruct((C, H, W), BF16), jax.ShapeDtypeStruct((C, H, W), BF16),
            jax.ShapeDtypeStruct((9, C + CC, C), F32),
            jax.ShapeDtypeStruct((9, C, C), F32), jax.ShapeDtypeStruct((9, C, C), F32),
        ),
        in_specs=[hbm, hbm],
        out_specs=(vmem,) * 5,
        scratch_shapes=[V((ROWS, C), BF16), pltpu.SemaphoreType.DMA((3,))],
        compiler_params=pltpu.CompilerParams(vmem_limit_bytes=60 * 1024 * 1024),
    )(fields, res)
    return field, grad_features, jnp.swapaxes(grad_in, 1, 2), grad_mid, grad_out


def solution(mesh):
    tile = P(None, "lat", "lon")
    in_specs = (
        tile, P("lon", "lat", None, None), P("lon", None, None, None), tile, tile,
        P(), P(), P(), P(), P(), P(), P(), tile,
    )
    out_specs = (tile, tile, P(), P(), P())
    return jax.shard_map(local, mesh=mesh, in_specs=in_specs, out_specs=out_specs, check_vma=False)
```

```python
import jax
import jax.numpy as jnp
from jax import lax
from jax.experimental import pallas as pl
from jax.experimental.pallas import tpu as pltpu
from jax.sharding import PartitionSpec as P

C = 128
CC = 40
G = 32
H = 8
W = 256
N = H * W
NP = N + 2 * W
BS = 256
SLOT = 8
NLON = 16
NLAT = 8
CELLS = 64 * 4096
MEMBERS = (C // G) * CELLS
FACTOR = CELLS ** -0.5
EPS = 1e-05
ROWS_IN = 96
ROWS_OM = 144
AT_OM = 0
AT_IN = AT_OM + 16 * ROWS_OM
ROWS = AT_IN + 16 * ROWS_IN
F32 = jnp.float32
BF16 = jnp.bfloat16
MESH = pl.DeviceIdType.MESH
FEAT, COT, COND, POOL, MERG, GMID, GIN = range(7)
HOPS = (0, 1, 2, 1)
OTHERS = sorted(
    [(a, b, c, d) for a in range(4) for b in range(4) for c in range(4) for d in range(2) if (a, b, c, d) != (0, 0, 0, 0)],
    key=lambda o: -(HOPS[o[0]] + HOPS[o[1]] + HOPS[o[2]]),
)


def dot(a, b):
    return lax.dot_general(a, b, (((1,), (0,)), ((), ())), preferred_element_type=F32)


def dot_nt(a, b):
    return lax.dot_general(a, b, (((1,), (1,)), ((), ())), preferred_element_type=F32)


def sigmoid(v):
    return 1.0 / (1.0 + jnp.exp(-v))


def kernel(
    feat, cot, blocks, table, src, wt, w_in, w_mid, w_out, gain_in, bias_in, gain_mid, bias_mid,
    fields, res,
    fc, relay, pool_s, pool_r, onehot, fid, fwt, acc, condf, hidden, gmerged, slope, act, merged, gin, up,
    x3f, x3c, x3m, x3g, x3cond, wf, wc, wo, wm, wt_out, wt_mid, wt_in,
    hr, hc, edge, crow, chr_, pooled, pooled_e, gmid, slope_r, slope_e, row_p, pack_p, row_g, pack_g, im_p, im_g,
    gsmall, a1, gw_in, s_in, s_om, core_in, core_om, half_in, half_om, r1_in, r1_om, r2_in, r2_om, full_in, full_om,
    sem_ps, sem_pr, sem_hs, sem_hr, sem_a, sem_b,
):
    lon = lax.axis_index("lon")
    lat = lax.axis_index("lat")

    def at(dlat, dlon):
        return {"lon": lax.rem(lon + dlon + NLON, NLON), "lat": lat + dlat}

    def has_lat(d):
        if d == 0:
            return None
        return jnp.logical_and(lat + d >= 0, lat + d < NLAT)

    def guarded(cond, fn):
        if cond is None:
            fn()
        else:
            pl.when(cond)(fn)

    finish = []

    def send(cond, source, dest, s_sem, r_sem, device):
        copy = pltpu.make_async_remote_copy(
            src_ref=source, dst_ref=dest, send_sem=s_sem, recv_sem=r_sem,
            device_id=device, device_id_type=MESH,
        )
        guarded(cond, copy.start)
        finish.append((cond, copy.wait_send))

    def arrive(ref, sem):
        pltpu.make_async_copy(ref, ref, sem).wait()

    barrier = pltpu.get_barrier_semaphore()

    core = lax.rem(lon, 2)
    chip = lon // 2
    x = lon // 4
    z = lat // 2
    y = lax.rem(chip, 2) * 2 + lax.rem(lat, 2)
    lon_of = {}
    lat_of = {}
    for oy in range(4):
        y2 = lax.rem(y + oy, 4)
        for oc in range(2):
            for ox in range(4):
                lon_of[ox, oy, oc] = (lax.rem(x + ox, 4) * 2 + y2 // 2) * 2 + (core if oc == 0 else 1 - core)
        for oz in range(4):
            lat_of[oz, oy] = lax.rem(z + oz, 4) * 2 + lax.rem(y2, 2)

    def everyone(act_on):
        for ox, oy, oz, oc in OTHERS:
            act_on({"lon": lon_of[ox, oy, oc], "lat": lat_of[oz, oy]})

    everyone(lambda peer: pl.semaphore_signal(barrier, inc=1, device_id=peer, device_id_type=MESH))

    def relaid(ref, base):
        cells = ref[...].astype(F32).reshape(C * H, W)
        for side in range(2):
            relay[side * C * H:(side + 1) * C * H] = cells[:, side * 128:(side + 1) * 128]
            for r in range(H):
                where = slice(r * W + side * 128, r * W + (side + 1) * 128)
                fc[base:base + C, where] = relay[pl.ds(side * C * H + r, C, stride=H), :].astype(BF16)

    relaid(feat, 0)
    relaid(cot, C)

    gaps = [0, 2, -2, 4, -4, 1, -1, 3, -3]

    def pack(k, dest):
        for s2 in range(0, 4, 2):
            for half in range(2):
                one = jnp.maximum(table[0, lat, lat + gaps[k], 2 * s2 + half], 0)
                two = jnp.maximum(table[0, lat, lat + gaps[k], 2 * s2 + 2 + half], 0)
                both = jnp.concatenate([blocks[0, one].astype(F32), blocks[0, two].astype(F32)], axis=0)
                dest[s2 * CC:(s2 + 2) * CC, half * BS:(half + 1) * BS] = both.astype(BF16)

    pack(0, pool_r.at[0])
    for k in range(1, 9):
        guarded(has_lat(gaps[k]), lambda k=k: pack(k, pool_s.at[k]))

    def edge_columns(ref, offset, chans, to):
        lanes = lax.broadcasted_iota(jnp.int32, (chans, 128), 1)
        tile = jnp.zeros((chans, 128), F32)
        for r in range(H):
            base = offset + r * W
            first = ref[:, base:base + 128].astype(F32)
            last = ref[:, base + 128:base + 256].astype(F32)
            tile = jnp.where(lanes == r + 1, first[:, 0:1], tile)
            tile = jnp.where(lanes == r + 17, last[:, 127:128], tile)
        if chans < C:
            tile = jnp.concatenate([tile, jnp.zeros((C - chans, 128), F32)], axis=0)
        to[...] = tile.T[0:32].astype(BF16)

    edge_columns(fc.at[0:C], 0, C, edge.at[FEAT])

    def make_onehot(j, _):
        m = j // H
        r = lax.rem(j, H)
        cells = src[m, pl.ds(r, 1), :]
        low = lax.rem(cells, 2 * BS)
        rows = lax.broadcasted_iota(jnp.int32, (2 * BS, W), 0)
        where = pl.ds(pl.multiple_of(j * W, W), W)
        onehot[:, where] = jnp.where(rows == low, 1.0, 0.0).astype(BF16)
        fid[:, where] = cells // (2 * BS)
        fwt[:, where] = wt[m, pl.ds(r, 1), :]
        return 0

    lax.fori_loop(0, 2 * H, make_onehot, 0)

    for r in range(H):
        small = lax.broadcasted_iota(jnp.int32, (C, W), 0)
        cell = lax.broadcasted_iota(jnp.int32, (C, W), 1)
        up[:, r * W:(r + 1) * W] = jnp.where(small == (r // 4) * 64 + cell // 4, 1.0, 0.0).astype(BF16)

    def turn(t):
        return t.astype(F32).T.astype(BF16)

    for a in range(3):
        rows = []
        for b in range(3):
            t = 3 * a + b
            wf[a, :, b * C:(b + 1) * C] = turn(w_in[t, 0:C, :])
            wo[a, :, b * C:(b + 1) * C] = w_out[t]
            wm[:, t * C:(t + 1) * C] = w_mid[t]
            rows.append(w_in[t, C:C + CC, :].astype(F32))
        wc[a] = jnp.concatenate(rows + [jnp.zeros((8, C), F32)], axis=0).T.astype(BF16)

    def turn_out():
        for t in range(9):
            wt_out[t // 3, :, (t % 3) * C:(t % 3 + 1) * C] = turn(w_out[8 - t])

    def turn_rest():
        for t in range(9):
            wt_mid[:, t * C:(t + 1) * C] = turn(w_mid[8 - t])
            wt_in[t // 3, :, (t % 3) * C:(t % 3 + 1) * C] = w_in[8 - t, 0:C, :]

    turn_out()

    pl.semaphore_wait(barrier, NLAT * NLON - 1)

    def send_fine(f, up_row, down_row, rows_at):
        send(has_lat(-1), up_row, rows_at.at[1], sem_hs.at[f, 0], sem_hr.at[f, 1], at(-1, 0))
        send(has_lat(1), down_row, rows_at.at[0], sem_hs.at[f, 1], sem_hr.at[f, 0], at(1, 0))
        for d in (0, -1, 1):
            left, right = edge.at[f, pl.ds(0, 16)], edge.at[f, pl.ds(16, 16)]
            send(has_lat(d), right, hc.at[f, pl.ds(16 - 16 * d, 16)], sem_hs.at[f, 3 + d], sem_hr.at[f, 3 - d], at(d, 1))
            send(has_lat(d), left, hc.at[f, pl.ds(64 - 16 * d, 16)], sem_hs.at[f, 6 + d], sem_hr.at[f, 6 - d], at(d, -1))

    def send_field(f, ref):
        send_fine(f, ref.at[:, 0:W], ref.at[:, N - W:N], hr.at[f])

    def expect(cond, ref, sem):
        if cond is None:
            arrive(ref, sem)
            return

        @pl.when(cond)
        def _():
            arrive(ref, sem)

        @pl.when(jnp.logical_not(cond))
        def _():
            ref[...] = jnp.zeros(ref.shape, ref.dtype)

    def wait_fine(f, rows_at):
        expect(has_lat(-1), rows_at.at[0], sem_hr.at[f, 0])
        expect(has_lat(1), rows_at.at[1], sem_hr.at[f, 1])
        for d in (0, -1, 1):
            expect(has_lat(d), hc.at[f, pl.ds(16 + 16 * d, 16)], sem_hr.at[f, 3 + d])
            expect(has_lat(d), hc.at[f, pl.ds(64 + 16 * d, 16)], sem_hr.at[f, 6 + d])
        cols = hc[f, 0:96, :].astype(F32)
        return jnp.concatenate([cols, jnp.zeros((32, C), F32)], axis=0).T

    def pool_copy(k):
        back = gaps.index(-gaps[k])
        return pltpu.make_async_remote_copy(
            src_ref=pool_s.at[k], dst_ref=pool_r.at[back], send_sem=sem_ps.at[k], recv_sem=sem_pr.at[back],
            device_id=at(gaps[k], 0), device_id_type=MESH,
        )

    for k in (5, 6, 7, 8, 1, 2, 3, 4):
        copy = pool_copy(k)
        guarded(has_lat(gaps[k]), copy.start)
        finish.append((has_lat(gaps[k]), copy.wait_send))
    send_field(FEAT, fc.at[0:C])

    def left_right(r, cols):
        if r == 0:
            return cols[:, 8:9], cols[:, 56:57]
        if r == H + 1:
            return cols[:, 33:34], cols[:, 81:82]
        return cols[:, 16 + r:17 + r], cols[:, 64 + r:65 + r]

    def shifted(v, r, cols):
        chans = v.shape[0]
        at_lane = lax.broadcasted_iota(jnp.int32, (chans, W), 1)
        first, last = left_right(r, cols)
        before = jnp.where(at_lane == 0, first, pltpu.roll(v, 1, 1))
        after = jnp.where(at_lane == W - 1, last, pltpu.roll(v, W - 1, 1))
        return before, after

    def build(x3, ref, rows_at, cols):
        for r in range(H + 2):
            if r == 0:
                v = rows_at[0]
            elif r == H + 1:
                v = rows_at[1]
            else:
                v = ref[:, (r - 1) * W:r * W]
            before, after = shifted(v.astype(F32), r, cols)
            x3[0:C, r * W:(r + 1) * W] = before.astype(BF16)
            x3[C:2 * C, r * W:(r + 1) * W] = v
            x3[2 * C:3 * C, r * W:(r + 1) * W] = after.astype(BF16)

    STEP = 1024

    def conv(weights, x3, use):
        def body(j, _):
            total = None
            for a in range(3):
                start = pl.multiple_of(j * STEP + a * W, W)
                part = dot(weights[a], x3[:, pl.ds(start, STEP)])
                total = part if total is None else total + part
            use(pl.ds(pl.multiple_of(j * STEP, STEP), STEP), total)
            return 0

        lax.fori_loop(0, N // STEP, body, 0)

    def put(ref):
        def use(where, v):
            ref[:, where] = v

        return use

    build(x3f, fc.at[0:C], hr.at[FEAT], wait_fine(FEAT, hr.at[FEAT]))
    conv(wf, x3f, put(hidden))
    def halves(v):
        high = v.astype(BF16)
        return high, (v - high.astype(F32)).astype(BF16)

    acc[...] = jnp.zeros(acc.shape, F32)

    def interp(k, _):
        size = lax.rem(2 * ((k + 1) // 2), 5)
        gap = jnp.where(lax.rem(k, 2) == 1, size, -size)
        owner = lat + gap

        @pl.when(jnp.logical_and(owner >= 0, owner < NLAT))
        def _():
            @pl.when(k > 0)
            def _():
                arrive(pool_r.at[k], sem_pr.at[k])

            products = dot(pool_r[k], onehot[...])
            total = acc[...]
            for s2 in range(4):
                mask = jnp.where(fid[...] == owner * 4 + s2, fwt[...], 0.0)
                total = total + products[s2 * CC:(s2 + 1) * CC] * mask
            acc[...] = total

        return 0

    lax.fori_loop(0, 9, interp, 0)

    blended = acc[:, 0:N] + acc[:, N:2 * N]
    condf[:, W:W + N] = blended.astype(BF16).astype(F32)
    edge_columns(condf, W, CC, edge.at[COND])
    for i, start in enumerate((W, N)):
        row = jnp.concatenate([condf[:, start:start + W], jnp.zeros((8, W), F32)], axis=0)
        crow[i] = row.astype(BF16)
    send_fine(COND, crow.at[0], crow.at[1], chr_)
    cond_cols = wait_fine(COND, chr_)[0:CC]
    for r in range(H + 2):
        if r == 0:
            v = chr_[0].astype(F32)[0:CC]
        elif r == H + 1:
            v = chr_[1].astype(F32)[0:CC]
        else:
            v = condf[:, r * W:(r + 1) * W]
        before, after = shifted(v, r, cond_cols)
        stacked = jnp.concatenate([before, v, after, jnp.zeros((8, W), F32)], axis=0)
        x3cond[:, r * W:(r + 1) * W] = stacked.astype(BF16)

    def add_hidden(where, v):
        hidden[:, where] = hidden[:, where] + v

    conv(wc, x3cond, add_hidden)

    chan = lax.broadcasted_iota(jnp.int32, (C, C), 0)
    other = lax.broadcasted_iota(jnp.int32, (C, C), 1)
    eye = chan == other
    to_first = jnp.where(other == chan // (C // G), 1.0, 0.0)
    to_second = jnp.where(other == G + chan // (C // G), 1.0, 0.0)
    me = lat * NLON + lon

    def to_row(col):
        return jnp.sum(jnp.where(eye, col, 0.0), axis=0, keepdims=True)

    def to_col(row):
        return jnp.sum(jnp.where(eye, row, 0.0), axis=1, keepdims=True)

    def all_sum(k, first, second, beside=None):
        one = jnp.sum(first, axis=1, keepdims=True)
        two = jnp.sum(second, axis=1, keepdims=True)
        mine = a1.at[k, pl.ds(me, 1)]
        a1[k, pl.ds(me, 1), :] = jnp.sum(one * to_first + two * to_second, axis=0, keepdims=True)

        def share(peer):
            pltpu.make_async_remote_copy(
                src_ref=mine, dst_ref=mine, send_sem=sem_a.at[k, 0], recv_sem=sem_a.at[k, 1],
                device_id=peer, device_id_type=MESH,
            ).start()

        everyone(share)
        if beside is not None:
            beside()
        rest = a1.at[k, pl.ds(0, NLAT * NLON - 1)]
        arrive(rest, sem_a.at[k, 1])
        finish.append((None, lambda: arrive(rest, sem_a.at[k, 0])))
        total = jnp.sum(a1[k], axis=0, keepdims=True)
        return (
            jnp.sum(total * to_first, axis=1, keepdims=True),
            jnp.sum(total * to_second, axis=1, keepdims=True),
        )

    def norm_terms(sums, squares, members):
        average = sums / members
        variance = squares / members - average * average
        return average, lax.rsqrt(variance + EPS)

    s = jnp.zeros((C, 128), F32)
    q = jnp.zeros((C, 128), F32)
    for j in range(N // 128):
        v = hidden[:, j * 128:(j + 1) * 128]
        s = s + v
        q = q + v * v
    def beside_first():
        edge_columns(fc.at[C:2 * C], 0, C, edge.at[COT])
        send_field(COT, fc.at[C:2 * C])
        turn_rest()

    sums, squares = all_sum(0, s, q, beside_first)
    avg_in, inv_in = norm_terms(sums, squares, MEMBERS)
    g1 = to_col(gain_in[...])
    b1 = to_col(bias_in[...])
    g2 = to_col(gain_mid[...])
    b2 = to_col(bias_mid[...])

    def activate(j, _):
        where = pl.ds(pl.multiple_of(j * W, W), W)
        affine = g1 * ((hidden[:, where] - avg_in) * inv_in) + b1
        act[:, where] = (affine * sigmoid(affine)).astype(BF16)
        return 0

    lax.fori_loop(0, H, activate, 0, unroll=True)

    def send_coarse(f, rows, near, mine, packs):
        half = rows.shape[0] // 2
        send(has_lat(-1), rows.at[pl.ds(0, half)], near.at[1], sem_hs.at[f, 0], sem_hr.at[f, 1], at(-1, 0))
        send(has_lat(1), rows.at[pl.ds(half, half)], near.at[0], sem_hs.at[f, 1], sem_hr.at[f, 0], at(1, 0))
        for d in (0, -1, 1):
            send(has_lat(d), mine, packs.at[1 - d], sem_hs.at[f, 3 + d], sem_hr.at[f, 3 - d], at(d, 1))
            send(has_lat(d), mine, packs.at[4 - d], sem_hs.at[f, 6 + d], sem_hr.at[f, 6 - d], at(d, -1))

    def wait_coarse(f, near, packs):
        expect(has_lat(-1), near.at[0], sem_hr.at[f, 0])
        expect(has_lat(1), near.at[1], sem_hr.at[f, 1])
        for d in (0, -1, 1):
            expect(has_lat(d), packs.at[1 + d], sem_hr.at[f, 3 + d])
            expect(has_lat(d), packs.at[4 + d], sem_hr.at[f, 6 + d])

    sub16 = lax.broadcasted_iota(jnp.int32, (16, C), 0)

    def corner_rows(v, first, base):
        for i, n in enumerate((0, 64, 63, 127)):
            base = jnp.where(sub16 == first + i, v[n:n + 1], base)
        return base

    def around(own, near, packs, part, first):
        size = 64
        above = near[0].astype(F32)[part * size:(part + 1) * size]
        below = near[1].astype(F32)[part * size:(part + 1) * size]
        full = jnp.concatenate([above, own, below], axis=0)
        ends = [packs[i].astype(F32) for i in range(6)]

        def row(i, n):
            return ends[i][first + n:first + n + 1]

        lefts = [row(0, 3), row(1, 2), row(1, 3), row(2, 2)]
        rights = [row(3, 1), row(4, 0), row(4, 1), row(5, 0)]
        return full, lefts, rights

    cells = lax.broadcasted_iota(jnp.int32, (2 * C, C), 0)

    def build_coarse(im, full, lefts, rights):
        before = pltpu.roll(full, 1, 0)
        after = pltpu.roll(full, 2 * C - 1, 0)
        for k in range(4):
            before = jnp.where(cells == 64 * k, lefts[k], before)
            after = jnp.where(cells == 64 * k + 63, rights[k], after)
        for b, v in enumerate((before, full, after)):
            v = v.astype(BF16)
            for a in range(3):
                im[:, (3 * a + b) * C:(3 * a + b + 1) * C] = v[a * 64:a * 64 + C]

    own = (dot_nt(up[...], act[...]) * (1.0 / 16.0)).astype(BF16)
    pooled[...] = own
    own = own.astype(F32)
    pooled_e[...] = corner_rows(own, 0, jnp.zeros((16, C), F32)).astype(BF16)
    send_coarse(POOL, pooled, row_p, pooled_e, pack_p)
    wait_coarse(POOL, row_p, pack_p)
    build_coarse(im_p, *around(own, row_p, pack_p, 0, 0))
    hidden_mid = dot_nt(wm[...], im_p[...])

    def beside_second():
        build(x3c, fc.at[C:2 * C], hr.at[COT], wait_fine(COT, hr.at[COT]))
        conv(wt_out, x3c, put(gmerged))
        high, low = halves(gmerged[...])
        gsmall[...] = dot_nt(high, up[...]) + dot_nt(low, up[...])

    sums, squares = all_sum(1, hidden_mid, hidden_mid * hidden_mid, beside_second)
    avg_mid, inv_mid = norm_terms(sums, squares, MEMBERS // 16)
    normed_mid = (hidden_mid - avg_mid) * inv_mid
    affine_mid = g2 * normed_mid + b2
    sig = sigmoid(affine_mid)
    act_mid = (affine_mid * sig).astype(BF16)
    slope_mid = gsmall[...] * sig * (1.0 + affine_mid * (1.0 - sig)) * g2
    slope_t = slope_mid.T
    normed_t = normed_mid.T

    def send_slopes():
        for i, n in enumerate((0, 64)):
            slope_r[i * C:i * C + 64] = slope_t[n:n + 64].astype(BF16)
            slope_r[i * C + 64:(i + 1) * C] = normed_t[n:n + 64].astype(BF16)
        ends = corner_rows(slope_t, 0, jnp.zeros((16, C), F32))
        slope_e[...] = corner_rows(normed_t, 4, ends).astype(BF16)
        send_coarse(GMID, slope_r, row_g, slope_e, pack_g)
        for r in range(H):
            where = slice(r * W, (r + 1) * W)
            merged[:, where] = (act[:, where].astype(F32) + dot(act_mid, up[:, where])).astype(BF16)
        edge_columns(merged, 0, C, edge.at[MERG])
        send_field(MERG, merged)

    sum_e, sum_en = all_sum(2, slope_mid, slope_mid * normed_mid, send_slopes)
    mean_e = sum_e / (MEMBERS // 16)
    mean_en = sum_en / (MEMBERS // 16)
    gmid[...] = ((slope_mid - mean_e - normed_mid * mean_en) * inv_mid).astype(BF16)
    wait_coarse(GMID, row_g, pack_g)
    row_e, row_en, row_inv = to_row(mean_e), to_row(mean_en), to_row(inv_mid)
    inside = [jnp.where(lat > 0, 1.0, 0.0), 1.0, 1.0, jnp.where(lat < NLAT - 1, 1.0, 0.0)]

    def settled(e, normed):
        return (e - row_e - normed * row_en) * row_inv

    e_all, e_left, e_right = around(slope_t, row_g, pack_g, 0, 0)
    n_all, n_left, n_right = around(normed_t, row_g, pack_g, 1, 4)
    valid = jnp.where(cells < 64, inside[0], jnp.where(cells < 192, 1.0, inside[3]))
    build_coarse(
        im_g,
        settled(e_all, n_all) * valid,
        [settled(e_left[k], n_left[k]) * inside[k] for k in range(4)],
        [settled(e_right[k], n_right[k]) * inside[k] for k in range(4)],
    )
    gpooled = dot_nt(wt_mid[...], im_g[...]) * (1.0 / 16.0)
    high, low = halves(gpooled)

    def slopes(j, carry):
        s, q = carry
        where = pl.ds(pl.multiple_of(j * W, W), W)
        gact = gmerged[:, where] + dot(high, up[:, where]) + dot(low, up[:, where])
        normed = (hidden[:, where] - avg_in) * inv_in
        affine = g1 * normed + b1
        sig = sigmoid(affine)
        e = gact * sig * (1.0 + affine * (1.0 - sig)) * g1
        slope[:, where] = e
        en = e * normed
        return s + e[:, 0:128] + e[:, 128:256], q + en[:, 0:128] + en[:, 128:256]

    s, q = lax.fori_loop(0, H, slopes, (jnp.zeros((C, 128), F32), jnp.zeros((C, 128), F32)), unroll=True)

    jobs = {
        0: (ROWS_OM, s_om, core_om, half_om, r1_om, r2_om, full_om),
        1: (ROWS_IN, s_in, core_in, half_in, r1_in, r2_in, full_in),
    }
    partner = {"lon": lon + 1 - 2 * core, "lat": lat}

    def pieces(ref, n):
        return ref.at[pl.ds(0, n)]

    def hand(k, step, source, dest, peer):
        pltpu.make_async_remote_copy(
            src_ref=source, dst_ref=dest, send_sem=sem_b.at[k, 2 * step], recv_sem=sem_b.at[k, 2 * step + 1],
            device_id=peer, device_id_type=MESH,
        ).start()

    def along_lon(d):
        return lax.rem(chip + d, NLON // 2)

    def cores(k):
        rows, s_ref, got = jobs[k][:3]
        part = pl.ds(pl.multiple_of((1 - core) * 8 * rows, 16), 8 * rows)
        hand(k, 0, s_ref.at[part], got, partner)
        finish.append((None, lambda: arrive(got, sem_b.at[k, 0])))

    def scatter(k):
        rows, s_ref, got, half, r1 = jobs[k][:5]
        arrive(got, sem_b.at[k, 1])
        part = pl.ds(pl.multiple_of(core * 8 * rows, 16), 8 * rows)
        half[...] = (s_ref[part, :].astype(F32) + got[...].astype(F32)).astype(BF16)
        for d in range(1, 8):
            to = along_lon(d)
            hand(k, 1, half.at[pl.ds(pl.multiple_of(to * rows, 16), rows)], r1.at[chip], {"lon": to * 2 + core, "lat": lat})
        r1[chip] = half[pl.ds(pl.multiple_of(chip * rows, 16), rows), :]
        finish.append((None, lambda: arrive(pieces(r1, 7), sem_b.at[k, 2])))

    def added(ref):
        total = ref[0].astype(F32)
        for i in range(1, 8):
            total = total + ref[i].astype(F32)
        return total.astype(BF16)

    def middle(k):
        r1, r2 = jobs[k][4:6]
        arrive(pieces(r1, 7), sem_b.at[k, 3])
        r2[lat] = added(r1)
        for d in range(1, NLAT):
            hand(k, 2, r2.at[lat], r2.at[lat], {"lon": lon, "lat": lax.rem(lat + d, NLAT)})
        finish.append((None, lambda: arrive(pieces(r2, 7), sem_b.at[k, 4])))

    def gather(k):
        r2, full = jobs[k][5:7]
        arrive(pieces(r2, 7), sem_b.at[k, 5])
        full[core, chip] = added(r2)
        for d in range(1, 8):
            hand(k, 3, full.at[core, chip], full.at[core, chip], {"lon": along_lon(d) * 2 + core, "lat": lat})
        finish.append((None, lambda: arrive(pieces(full.at[core], 7), sem_b.at[k, 6])))

    def exchange(k):
        full = jobs[k][6]
        arrive(pieces(full.at[core], 7), sem_b.at[k, 7])
        hand(k, 4, full.at[core], full.at[core], partner)
        finish.append((None, lambda: arrive(full.at[core], sem_b.at[k, 8])))

    def complete(k, base):
        rows, full = jobs[k][0], jobs[k][6]
        arrive(full.at[1 - core], sem_b.at[k, 9])
        res[base:base + 16 * rows] = full[...].reshape(16 * rows, C)

    def beside_slopes():
        build(x3m, merged, hr.at[MERG], wait_fine(MERG, hr.at[MERG]))
        for a in range(3):
            part = dot_nt(fc[C:2 * C], x3m[:, a * W:a * W + N])
            for b in range(3):
                t = 9 + 3 * a + b
                s_om[t * C:(t + 1) * C] = part[:, b * C:(b + 1) * C].astype(BF16)
        g_mid_w = dot(gmid[...], im_p[...])
        for t in range(9):
            s_om[t * C:(t + 1) * C] = g_mid_w[:, t * C:(t + 1) * C].astype(BF16)
        cores(0)

    sum_e, sum_en = all_sum(3, s, q, beside_slopes)
    scatter(0)
    mean_e = sum_e / MEMBERS
    mean_en = sum_en / MEMBERS

    def finish_in(j, _):
        where = pl.ds(pl.multiple_of(j * W, W), W)
        normed = (hidden[:, where] - avg_in) * inv_in
        gin[:, where] = ((slope[:, where] - mean_e - normed * mean_en) * inv_in).astype(BF16)
        return 0

    lax.fori_loop(0, H, finish_in, 0, unroll=True)

    taps = C + CC
    for a in range(3):
        part = dot_nt(x3f[:, a * W:a * W + N], gin[...])
        more = dot_nt(x3cond[:, a * W:a * W + N], gin[...])
        for b in range(3):
            t = 3 * a + b
            gw_in[t * taps:t * taps + C] = part[b * C:(b + 1) * C]
            gw_in[t * taps + C:(t + 1) * taps] = more[b * CC:(b + 1) * CC]
    gw_in[9 * taps:] = jnp.zeros((16 * ROWS_IN - 9 * taps, C), F32)
    s_in[...] = gw_in[...].astype(BF16)
    cores(1)
    edge_columns(gin, 0, C, edge.at[GIN])
    send_field(GIN, gin)
    scatter(1)

    def put_relaid(where, v):
        for i in range(STEP // 128):
            first = (i % 2) * C * H + where.start // W + i // 2
            relay[pl.ds(first, C, stride=H), :] = v[:, i * 128:(i + 1) * 128]

    def put_field(base):
        for side in range(2):
            cells = relay[side * C * H:(side + 1) * C * H].reshape(C, H, 128)
            fields[base:base + C, :, side * 128:(side + 1) * 128] = cells.astype(BF16)

    def put_out(where, v):
        put_relaid(where, fc[0:C, where].astype(F32) + v)

    conv(wo, x3m, put_out)
    put_field(0)
    middle(0)
    middle(1)
    build(x3g, gin, hr.at[GIN], wait_fine(GIN, hr.at[GIN]))

    def put_feat(where, v):
        put_relaid(where, fc[C:2 * C, where].astype(F32) + v)

    gather(0)
    conv(wt_in, x3g, put_feat)
    put_field(C)
    gather(1)
    exchange(0)
    complete(0, AT_OM)
    exchange(1)
    complete(1, AT_IN)
    for cond, wait in finish:
        guarded(cond, wait)


def results(fields, res_h, field, features, grad_in, grad_mid, grad_out, res, sem):
    moves = [
        pltpu.make_async_copy(a, b, sem.at[i])
        for i, (a, b) in enumerate(((res_h, res), (fields.at[0:C], field), (fields.at[C:2 * C], features)))
    ]
    for move in moves:
        move.start()
    moves[0].wait()
    for t in range(9):
        rows = slice(AT_IN + t * (C + CC), AT_IN + (t + 1) * (C + CC))
        grad_in[t] = res[rows].astype(F32) * FACTOR
        grad_mid[t] = res[AT_OM + t * C:AT_OM + (t + 1) * C].astype(F32) * FACTOR
        grad_out[t] = res[AT_OM + (9 + t) * C:AT_OM + (10 + t) * C].astype(F32) * FACTOR
    for move in moves[1:]:
        move.wait()


def local(
    features, coarse_blocks, send_table, interp_src, interp_wt, weight_in, weight_mid, weight_out,
    gain_in, bias_in, gain_mid, bias_mid, cotangent,
):
    vmem = pl.BlockSpec(memory_space=pltpu.VMEM)
    smem = pl.BlockSpec(memory_space=pltpu.SMEM)
    hbm = pl.BlockSpec(memory_space=pltpu.HBM)
    V = pltpu.VMEM
    scratch = [
        V((2 * C, N), BF16), V((2 * C * H, 128), F32),
        V((9, 4 * CC, 2 * BS), BF16), V((9, 4 * CC, 2 * BS), BF16), V((2 * BS, 2 * N), BF16),
        V((1, 2 * N), jnp.int32), V((1, 2 * N), F32),
        V((CC, 2 * N), F32), V((CC, NP), F32), V((C, N), F32), V((C, N), F32), V((C, N), F32),
        V((C, N), BF16), V((C, N), BF16), V((C, N), BF16), V((C, N), BF16),
        V((3 * C, NP), BF16), V((3 * C, NP), BF16), V((3 * C, NP), BF16), V((3 * C, NP), BF16), V((C, NP), BF16),
        V((3, C, 3 * C), BF16), V((3, C, C), BF16), V((3, C, 3 * C), BF16), V((C, 9 * C), BF16),
        V((3, C, 3 * C), BF16), V((C, 9 * C), BF16), V((3, C, 3 * C), BF16),
        V((7, 2, C, W), BF16), V((7, C, C), BF16), V((7, 32, C), BF16), V((2, 48, W), BF16), V((2, 48, W), BF16),
        V((C, C), BF16), V((16, C), BF16), V((C, C), BF16), V((2 * C, C), BF16), V((16, C), BF16),
        V((2, 64, C), BF16), V((6, 16, C), BF16), V((2, C, C), BF16), V((6, 16, C), BF16),
        V((C, 9 * C), BF16), V((C, 9 * C), BF16),
        V((C, C), F32), V((4, NLAT * NLON, C), F32), V((16 * ROWS_IN, C), F32),
        V((16 * ROWS_IN, C), BF16), V((16 * ROWS_OM, C), BF16), V((8 * ROWS_IN, C), BF16), V((8 * ROWS_OM, C), BF16),
        V((8 * ROWS_IN, C), BF16), V((8 * ROWS_OM, C), BF16), V((8, ROWS_IN, C), BF16), V((8, ROWS_OM, C), BF16),
        V((8, ROWS_IN, C), BF16), V((8, ROWS_OM, C), BF16), V((2, 8, ROWS_IN, C), BF16), V((2, 8, ROWS_OM, C), BF16),
        pltpu.SemaphoreType.DMA((9,)), pltpu.SemaphoreType.DMA((9,)),
        pltpu.SemaphoreType.DMA((7, 8)), pltpu.SemaphoreType.DMA((7, 8)),
        pltpu.SemaphoreType.DMA((4, 2)), pltpu.SemaphoreType.DMA((2, 10)),
    ]
    fields, res = pl.pallas_call(
        kernel,
        out_shape=(jax.ShapeDtypeStruct((2 * C, H, W), BF16), jax.ShapeDtypeStruct((ROWS, C), BF16)),
        in_specs=[vmem, vmem, vmem, smem] + [vmem] * 9,
        out_specs=(vmem, vmem),
        scratch_shapes=scratch,
        compiler_params=pltpu.CompilerParams(
            collective_id=0, has_side_effects=True, vmem_limit_bytes=56 * 1024 * 1024
        ),
    )(
        features, cotangent, coarse_blocks, send_table, interp_src, interp_wt, jnp.swapaxes(weight_in, 1, 2), weight_mid, weight_out,
        gain_in.reshape(1, C), bias_in.reshape(1, C), gain_mid.reshape(1, C), bias_mid.reshape(1, C),
    )
    field, grad_features, grad_in, grad_mid, grad_out = pl.pallas_call(
        results,
        out_shape=(
            jax.ShapeDtypeStruct((C, H, W), BF16), jax.ShapeDtypeStruct((C, H, W), BF16),
            jax.ShapeDtypeStruct((9, C + CC, C), F32),
            jax.ShapeDtypeStruct((9, C, C), F32), jax.ShapeDtypeStruct((9, C, C), F32),
        ),
        in_specs=[hbm, hbm],
        out_specs=(vmem,) * 5,
        scratch_shapes=[V((ROWS, C), BF16), pltpu.SemaphoreType.DMA((3,))],
        compiler_params=pltpu.CompilerParams(vmem_limit_bytes=60 * 1024 * 1024),
    )(fields, res)
    return field, grad_features, jnp.swapaxes(grad_in, 1, 2), grad_mid, grad_out


def solution(mesh):
    tile = P(None, "lat", "lon")
    in_specs = (
        tile, P("lon", "lat", None, None), P("lon", None, None, None), tile, tile,
        P(), P(), P(), P(), P(), P(), P(), tile,
    )
    out_specs = (tile, tile, P(), P(), P())
    return jax.shard_map(local, mesh=mesh, in_specs=in_specs, out_specs=out_specs, check_vma=False)
```
